256 devices in a mesh: row: 32 (over z_hi, x, y), col: 8 (over z_lo, core).
Axes of the slice: x: 4, y: 4, z: 8 (z_hi: 2, z_lo: 4; z = z_hi * 4 + z_lo), core: 2. Of those that a mesh axis runs over, the one named last changes fastest.
Arguments:
- features: bfloat16 [256, 32, 64, 128], P('row', None, 'col'), may hold values from -6 to 6
- down_weight: bfloat16 [4, 4, 4, 32, 512], replicated, may hold values from -0.25 to 0.25
- bott_weight: bfloat16 [3, 3, 3, 512, 512], P(None, None, None, 'row'), may hold values from -0.078125 to 0.078125
- up_weight: bfloat16 [4, 4, 4, 32, 512], replicated, may hold values from -0.375 to 0.375
- dec_weight: bfloat16 [3, 3, 3, 32, 32], replicated, may hold values from -0.21875 to 0.21875
Outputs:
- decoded: bfloat16 [256, 32, 64, 128], P('row', None, 'col')
The draws below stay inside these ranges and needn't reach their ends.
All inputs are finite; a program needn't handle non-finite values.
Results may differ from the reference program's by a relative error of at most 0.015.
Values may be sent and summed in bfloat16 or wider, within the bound.
A program may use at most 128 MiB of HBM per device.

```python
import jax
import jax.numpy as jnp
from jax import lax

C1 = 32
CB = 512
WIDTH = 128
DEPTH = 256
HEIGHT = 64


def steps_of(own_key, dims, split, least, top_value):
    gain = 1.0
    for dim, blocks in split:
        draws = jax.random.uniform(jax.random.fold_in(jax.random.fold_in(own_key, 6), dim), (blocks,), jnp.float32, least / len(split), top_value / len(split))
        gain = gain * jnp.repeat(jnp.exp(draws), dims[dim] // blocks).reshape((-1,) + (1,) * (len(dims) - 1 - dim))
    return gain


def normal_values(rng, dims, spread, most, shards=(), kind=jnp.bfloat16):
    level = steps_of(rng, dims, shards, -0.22, 0.18) if shards else 1.0
    values = jax.random.normal(rng, dims, jnp.float32) * spread * level
    return jnp.minimum(jnp.maximum(values, -most), most).astype(kind)


def setup_inputs(seed: int = 0) -> dict:
    key_list = jax.random.split(jax.random.key(seed), 6)
    features = normal_values(key_list[0], (DEPTH, C1, HEIGHT, WIDTH), 1.0, 6.0, ((0, 32), (2, 8)))
    down_weight = normal_values(key_list[1], (4, 4, 4, C1, CB), (16 * C1) ** -0.5, 0.25)
    bott_weight = normal_values(key_list[2], (3, 3, 3, CB, CB), (27 * CB // 2) ** -0.5, 0.078125, ((3, 32),))
    up_weight = normal_values(key_list[3], (4, 4, 4, C1, CB), (CB // 2) ** -0.5, 0.375)
    dec_weight = normal_values(key_list[4], (3, 3, 3, C1, C1), (27 * C1) ** -0.5, 0.21875)
    return {"features": features, "down_weight": down_weight, "bott_weight": bott_weight, "up_weight": up_weight, "dec_weight": dec_weight}


def convolve(field, kernel):
    return lax.conv_general_dilated(field[None].astype(jnp.float32), kernel.astype(jnp.float32), (1, 1, 1), ((1, 1), (1, 1), (1, 1)), dimension_numbers=("NDCHW", "DHWIO", "NDCHW"), precision=lax.Precision.HIGHEST, preferred_element_type=jnp.float32)[0]


def reference(features, down_weight, bott_weight, up_weight, dec_weight):
    depth, chans, height, width = features.shape
    pooled = features.astype(jnp.float32).reshape(depth // 2, 2, chans, height // 2, 2, width // 2, 2).mean(axis=(1, 4, 6)).astype(jnp.bfloat16)
    blocks = pooled.astype(jnp.float32).reshape(depth // 8, 4, chans, height // 8, 4, width // 8, 4)
    lowered = jax.nn.silu(jnp.einsum("daihbwc,abcio->dohw", blocks, down_weight.astype(jnp.float32), precision=lax.Precision.HIGHEST)).astype(jnp.bfloat16)
    middle = jax.nn.silu(convolve(lowered, bott_weight)).astype(jnp.bfloat16)
    raised = jnp.einsum("dihw,abcoi->daohbwc", middle.astype(jnp.float32), up_weight.astype(jnp.float32), precision=lax.Precision.HIGHEST)
    raised = raised.reshape(depth // 2, chans, height // 2, width // 2)
    raised = jnp.repeat(jnp.repeat(jnp.repeat(raised, 2, axis=0), 2, axis=2), 2, axis=3)
    joined = (features.astype(jnp.float32) + raised).astype(jnp.bfloat16)
    return jax.nn.silu(convolve(joined, dec_weight)).astype(jnp.bfloat16)
```

```python
import jax
import jax.numpy as jnp
from jax import lax
from jax.experimental import pallas as pl
from jax.experimental.pallas import tpu as pltpu
from jax.sharding import PartitionSpec as P

MESH = pl.DeviceIdType.MESH
F32 = jnp.float32
BF16 = jnp.bfloat16
ROWS, COLS, GROUP = 32, 8, 4
C1, CB, WIDTH = 32, 512, 128
DEP, HGT, WB = 8, 8, 16
CIN = CB // ROWS
NT = (((1,), (1,)), ((), ()))


def iota(shape, dim):
    return lax.broadcasted_iota(jnp.int32, shape, dim)


def ones_where(mask):
    return jnp.where(mask, 1.0, 0.0).astype(BF16)


def silu(v):
    return v / (1.0 + jnp.exp(-v))


def dot(a, b):
    return jnp.dot(a, b, preferred_element_type=F32)


def dot_nt(a, b):
    return lax.dot_general(a, b, NT, preferred_element_type=F32)


def kernel(
    feat_hbm, down_hbm, bott_hbm, up_hbm, dec_hbm, out_ref,
    feat, down, up, dec, wg, lowered, tiles, part, arrived, band, band_h,
    slabs, edges_out, edges_in, edges, accs,
    load_sem, w_send, w_recv, a_send, a_recv, h_send, h_recv, p_send, p_recv, j_send, j_recv,
):
    row, col = lax.axis_index("row"), lax.axis_index("col")
    lane = row % GROUP
    half = (row // GROUP) % 2

    def at_row(step):
        return (row + step + ROWS) % ROWS

    def at_col(step):
        return (col + step + COLS) % COLS

    def device(r, c):
        return {"row": r, "col": c}

    loads = [
        pltpu.make_async_copy(src, dst, load_sem.at[i])
        for i, (src, dst) in enumerate(
            [(feat_hbm, feat), (down_hbm, down), (dec_hbm, dec), (up_hbm, up)]
        )
    ]
    for load in loads:
        load.start()

    def weight_slot(owner_lane):
        start = pl.multiple_of(half * (GROUP * CIN) + owner_lane * CIN, CIN)
        return wg.at[:, pl.ds(start, CIN), :]

    def weight_piece(lane_to):
        return bott_hbm.at[:, :, pl.ds(pl.multiple_of(lane_to * 128, 128), 128)]

    own_weight = pltpu.make_async_copy(weight_piece(lane), weight_slot(lane), load_sem.at[4])
    own_weight.start()

    barrier = pltpu.get_barrier_semaphore()

    def greet(r, c):
        pl.semaphore_signal(barrier, inc=1, device_id=device(r, c), device_id_type=MESH)

    @pl.loop(1, ROWS)
    def _(j):
        greet(at_row(j), col)

    for dr in (-1, 0, 1):
        for dc in (-1, 1):
            greet(at_row(dr), at_col(dc))

    rest = pl.multiple_of((1 - half) * (GROUP * CIN), GROUP * CIN)
    wg[:, pl.ds(rest, GROUP * CIN), :] = jnp.zeros((27, GROUP * CIN, 128), BF16)
    tiles[:, 0] = jnp.zeros((3, WB, 128), BF16)
    tiles[:, ROWS + 1] = jnp.zeros((3, WB, 128), BF16)

    loads[0].wait()
    r_, c_ = iota((128, 256), 0), iota((128, 256), 1)
    pool_h = ones_where(((r_ % C1) == (c_ // HGT)) & ((r_ // C1) == (c_ % HGT) // 2))
    pool_h = jnp.concatenate([pool_h, pool_h], axis=1)
    r_, c_ = iota((64, WIDTH), 0), iota((64, WIDTH), 1)
    pool_w = jnp.where((c_ // 2) == (r_ % WB) * 4 + r_ // WB, 0.125, 0.0).astype(BF16)
    pooled = []
    for a in range(4):
        pair = feat[2 * a : 2 * a + 2].reshape(512, WIDTH)
        pooled.append(dot_nt(pool_w, dot(pool_h, pair).astype(BF16)).astype(BF16))
    pooled = jnp.concatenate(pooled, axis=1)

    pl.semaphore_wait(barrier, ROWS - 1 + 6)

    weight_sends = []
    for j in range(1, GROUP):
        to = (lane + j) % GROUP
        copy = pltpu.make_async_remote_copy(
            src_ref=weight_piece(to),
            dst_ref=weight_slot(lane),
            send_sem=w_send.at[j - 1],
            recv_sem=w_recv.at[j - 1],
            device_id=device(row - lane + to, col),
            device_id_type=MESH,
        )
        copy.start()
        weight_sends.append(copy)

    loads[1].wait()
    total = jnp.zeros((WB, CB), F32)
    for c in range(4):
        total += dot(pooled[c * WB : (c + 1) * WB], down[:, c].reshape(512, CB))
    low = silu(total).astype(BF16)
    for k in range(4):
        lowered[k] = low[:, k * 128 : (k + 1) * 128]

    def tile_copy(j):
        to = at_row(j)
        return pltpu.make_async_remote_copy(
            src_ref=lowered.at[to // 8],
            dst_ref=tiles.at[1, 1 + row],
            send_sem=a_send,
            recv_sem=a_recv,
            device_id=device(to, col),
            device_id_type=MESH,
        )

    @pl.loop(1, ROWS)
    def _(j):
        tile_copy(j).start()

    tiles[1, 1 + row] = lowered[row // 8]

    loads[2].wait()
    r_, c_ = iota((256, C1), 0), iota((256, C1), 1)
    spread_o = ones_where((r_ // HGT) == c_)
    r_, c_ = iota((C1, 256), 0), iota((C1, 256), 1)
    spread_c = ones_where((c_ // HGT) == r_)
    shift = (iota((256, 256), 1) % HGT) - (iota((256, 256), 0) % HGT)
    h_of = iota((256, C1), 0) % HGT
    for kd in range(3):
        for kw in range(3):
            total = jnp.zeros((256, 256), F32)
            sides = []
            for kh in range(3):
                taps = dot_nt(spread_o, dec[(kd * 3 + kh) * 3 + kw]).astype(BF16)
                total = jnp.where(shift == kh - 1, dot(taps, spread_c), total)
                if kh != 1:
                    edge = 0 if kh == 0 else HGT - 1
                    sides.append(jnp.where(h_of == edge, taps.astype(F32), 0.0))
            at = kd * 3 + kw
            band[:, at * 256 : (at + 1) * 256] = total.astype(BF16)
            band_h[:, at * 64 : (at + 1) * 64] = jnp.concatenate(sides, axis=1).astype(BF16)

    def all_tiles(ref, send, recv):
        span = ref.at[pl.ds(1, ROWS - 1)]
        return pltpu.make_async_remote_copy(
            src_ref=span, dst_ref=span, send_sem=send, recv_sem=recv,
            device_id=device(at_row(1), col), device_id_type=MESH,
        )

    all_tiles(tiles.at[1], a_send, a_recv).wait_recv()

    halo_sends = []
    for i, step in enumerate((-1, 1)):
        copy = pltpu.make_async_remote_copy(
            src_ref=tiles.at[1, pl.ds(1, ROWS)],
            dst_ref=tiles.at[1 - step, pl.ds(1, ROWS)],
            send_sem=h_send.at[i],
            recv_sem=h_recv.at[i],
            device_id=device(row, at_col(step)),
            device_id_type=MESH,
        )
        copy.start()
        halo_sends.append(copy)

    own_weight.wait()
    for copy in weight_sends:
        copy.wait()

    def patches(heights):
        return jnp.concatenate(
            [tiles[b, a : a + ROWS].reshape(ROWS * WB, 128) for a in range(3) for b in heights], axis=1
        )

    def taps_of(heights):
        return jnp.concatenate(
            [
                jnp.concatenate([wg[a * 9 + b * 3 + c] for a in range(3) for b in heights], axis=0)
                for c in range(3)
            ],
            axis=1,
        )

    partial = dot(patches((1,)), taps_of((1,)))
    for copy in halo_sends:
        copy.wait()

    @pl.when(col == 0)
    def _():
        tiles[0] = jnp.zeros((ROWS + 2, WB, 128), BF16)

    @pl.when(col == COLS - 1)
    def _():
        tiles[2] = jnp.zeros((ROWS + 2, WB, 128), BF16)

    partial += dot(patches((0, 2)), taps_of((0, 2)))
    w_of = iota((ROWS * WB, 128), 0) % WB
    before = pltpu.roll(partial[:, :128], 1, 0)
    after = pltpu.roll(partial[:, 256:], ROWS * WB - 1, 0)
    summed = partial[:, 128:256] + jnp.where(w_of == 0, 0.0, before) + jnp.where(w_of == WB - 1, 0.0, after)
    part[...] = summed.astype(BF16).reshape(ROWS, WB, 128)

    def part_copy(j):
        to = at_row(j)
        return pltpu.make_async_remote_copy(
            src_ref=part.at[to],
            dst_ref=arrived.at[row],
            send_sem=p_send,
            recv_sem=p_recv,
            device_id=device(to, col),
            device_id_type=MESH,
        )

    @pl.loop(1, ROWS)
    def _(j):
        part_copy(j).start()

    arrived[row] = part[row]
    r_, c_ = iota((512, WB), 0), iota((512, WB), 1)
    spread_w = ones_where((((r_ % WIDTH) // 8) == c_) & ((((r_ % WIDTH) // 2) % 4) == (r_ // WIDTH)))
    r_, c_ = iota((256, 128), 0), iota((256, 128), 1)
    raise_h = ones_where(((c_ % C1) == (r_ // HGT)) & ((c_ // C1) == (r_ % HGT) // 2))
    loads[3].wait()
    all_tiles(arrived, p_send, p_recv).wait_recv()

    groups = arrived[...].reshape(ROWS // GROUP, GROUP, WB, 128).astype(F32).sum(axis=0)
    middle = silu(jnp.concatenate([groups[k] for k in range(GROUP)], axis=1)).astype(BF16)
    spread = dot(spread_w, middle).astype(BF16)
    raised = jnp.zeros((512, WIDTH), F32)
    for c in range(4):
        raised += dot_nt(up[:, c].reshape(512, CB), spread[c * WIDTH : (c + 1) * WIDTH])
    raised = raised.astype(BF16)

    v_of = iota((256, WIDTH), 1)

    def store_slab(i, value, rows=256):
        v_ = v_of[:rows]
        return (
            jnp.where(v_ == 0, 0.0, pltpu.roll(value, 1, 1)).astype(BF16),
            jnp.where(v_ == WIDTH - 1, 0.0, pltpu.roll(value, WIDTH - 1, 1)).astype(BF16),
        )

    r_, c_ = iota((64, 256), 0), iota((64, 256), 1)
    pick = ones_where(((c_ // HGT) == (r_ % C1)) & ((c_ % HGT) == (r_ // C1) * (HGT - 1)))
    for d in range(DEP):
        if d % 2 == 0:
            lift = dot(raise_h, raised[(d // 2) * 128 : (d // 2 + 1) * 128])
        joined = (feat[d].astype(F32) + lift).astype(BF16)
        slabs[1 + d, 1] = joined
        rim = dot(pick, joined).astype(BF16)
        edges_out[0, d] = rim[:C1]
        edges_out[1, d] = rim[C1:]

    moves = []
    for side, step in ((0, -1), (1, 1)):
        moves.append((edges_out.at[side], edges_in.at[1 - side, pl.ds(1, DEP)], row, at_col(step)))
        for d, hop, slot in ((0, -1, DEP + 1), (DEP - 1, 1, 0)):
            moves.append((edges_out.at[side, d], edges_in.at[1 - side, slot], at_row(hop), at_col(step)))
    for d, hop, slot in ((1, -1, DEP + 1), (DEP, 1, 0)):
        moves.append((slabs.at[d, 1], slabs.at[slot, 1], at_row(hop), col))
    joined_sends = []
    for i, (src, dst, r, c) in enumerate(moves):
        copy = pltpu.make_async_remote_copy(
            src_ref=src, dst_ref=dst, send_sem=j_send.at[i], recv_sem=j_recv.at[i],
            device_id=device(r, c), device_id_type=MESH,
        )
        copy.start()
        joined_sends.append(copy)

    for d in range(1, DEP + 1):
        left, right = store_slab(d, slabs[d, 1].astype(F32))
        slabs[d, 0] = left
        slabs[d, 2] = right
    for d in range(1, DEP - 1):
        accs[d] = dot(band[...], slabs[d : d + 3].reshape(9 * 256, WIDTH))

    for copy in joined_sends:
        copy.wait()

    @pl.when(row == 0)
    def _():
        slabs[0, 1] = jnp.zeros((256, WIDTH), BF16)
        edges_in[:, 0] = jnp.zeros((2, C1, WIDTH), BF16)

    @pl.when(row == ROWS - 1)
    def _():
        slabs[DEP + 1, 1] = jnp.zeros((256, WIDTH), BF16)
        edges_in[:, DEP + 1] = jnp.zeros((2, C1, WIDTH), BF16)

    @pl.when(col == 0)
    def _():
        edges_in[0] = jnp.zeros((DEP + 2, C1, WIDTH), BF16)

    @pl.when(col == COLS - 1)
    def _():
        edges_in[1] = jnp.zeros((DEP + 2, C1, WIDTH), BF16)

    for d in (0, DEP + 1):
        left, right = store_slab(d, slabs[d, 1].astype(F32))
        slabs[d, 0] = left
        slabs[d, 2] = right
    for d in range(DEP + 2):
        rim = jnp.concatenate([edges_in[0, d], edges_in[1, d]], axis=0)
        left, right = store_slab(d, rim.astype(F32), 64)
        edges[d, 0] = left
        edges[d, 1] = rim
        edges[d, 2] = right
    for d in range(DEP):
        if d in (0, DEP - 1):
            total = dot(band[...], slabs[d : d + 3].reshape(9 * 256, WIDTH))
        else:
            total = accs[d]
        total += dot(band_h[...], edges[d : d + 3].reshape(9 * 64, WIDTH))
        out_ref[d] = silu(total).astype(BF16)

    all_tiles(tiles.at[1], a_send, a_recv).wait_send()
    all_tiles(arrived, p_send, p_recv).wait_send()


def body(features, down_weight, bott_weight, up_weight, dec_weight):
    dma = pltpu.SemaphoreType.DMA
    out = pl.pallas_call(
        kernel,
        out_shape=jax.ShapeDtypeStruct((DEP, 256, WIDTH), BF16),
        in_specs=[pl.BlockSpec(memory_space=pl.ANY)] * 5,
        out_specs=pl.BlockSpec(memory_space=pltpu.VMEM),
        scratch_shapes=[
            pltpu.VMEM((DEP, 256, WIDTH), BF16),
            pltpu.VMEM((16, 4, C1, CB), BF16),
            pltpu.VMEM((16, 4, C1, CB), BF16),
            pltpu.VMEM((27, C1, C1), BF16),
            pltpu.VMEM((27, 128, 128), BF16),
            pltpu.VMEM((4, WB, 128), BF16),
            pltpu.VMEM((3, ROWS + 2, WB, 128), BF16),
            pltpu.VMEM((ROWS, WB, 128), BF16),
            pltpu.VMEM((ROWS, WB, 128), BF16),
            pltpu.VMEM((256, 9 * 256), BF16),
            pltpu.VMEM((256, 9 * 64), BF16),
            pltpu.VMEM((DEP + 2, 3, 256, WIDTH), BF16),
            pltpu.VMEM((2, DEP, C1, WIDTH), BF16),
            pltpu.VMEM((2, DEP + 2, C1, WIDTH), BF16),
            pltpu.VMEM((DEP + 2, 3, 64, WIDTH), BF16),
            pltpu.VMEM((DEP, 256, WIDTH), F32),
            dma((5,)), dma((3,)), dma((3,)), dma, dma, dma((2,)), dma((2,)), dma, dma, dma((8,)), dma((8,)),
        ],
        compiler_params=pltpu.CompilerParams(
            collective_id=0, has_side_effects=True, vmem_limit_bytes=48 * 1024 * 1024
        ),
        name="encode_decode",
    )(
        features.reshape(DEP, 256, WIDTH),
        down_weight.reshape(16, 4, C1, CB),
        bott_weight.reshape(27, CIN, CB),
        up_weight.reshape(16, 4, C1, CB),
        dec_weight.reshape(27, C1, C1),
    )
    return out.reshape(features.shape)


def solution(mesh):
    placed = (P("row", None, "col", None), P(), P(None, None, None, "row", None), P(), P())
    return jax.shard_map(
        body, mesh=mesh, in_specs=placed, out_specs=P("row", None, "col", None), check_vma=False
    )
```

```python
import jax
import jax.numpy as jnp
from jax import lax
from jax.experimental import pallas as pl
from jax.experimental.pallas import tpu as pltpu
from jax.sharding import PartitionSpec as P

MESH = pl.DeviceIdType.MESH
F32 = jnp.float32
BF16 = jnp.bfloat16
ROWS, COLS, GROUP = 32, 8, 4
C1, CB, WIDTH = 32, 512, 128
DEP, HGT, WB = 8, 8, 16
CIN = CB // ROWS
NT = (((1,), (1,)), ((), ()))


def iota(shape, dim):
    return lax.broadcasted_iota(jnp.int32, shape, dim)


def ones_where(mask):
    return jnp.where(mask, 1.0, 0.0).astype(BF16)


def silu(v):
    return v / (1.0 + jnp.exp(-v))


def dot(a, b):
    return jnp.dot(a, b, preferred_element_type=F32)


def dot_nt(a, b):
    return lax.dot_general(a, b, NT, preferred_element_type=F32)


def hops(offset):
    dz, dx, dy = offset
    return 4 * dz + min(dx, 4 - dx) + min(dy, 4 - dy)


PEERS = sorted(
    [(dz, dx, dy) for dz in range(2) for dx in range(4) for dy in range(4) if dz + dx + dy],
    key=hops,
    reverse=True,
)


def kernel(
    feat_hbm, down_hbm, bott_hbm, up_hbm, dec_hbm, out_ref,
    feat, down, up, dec, wg, lowered, tiles, part, arrived, band, band_h,
    slabs, edges_out, edges_in, edges, accs, feat_in, raised_out, raised_in,
    load_sem, w_send, w_recv, a_send, a_recv, h_send, h_recv, p_send, p_recv, j_send, j_recv, f_send, f_recv,
):
    row, col = lax.axis_index("row"), lax.axis_index("col")
    row_z, row_x, lane = row // 16, (row // GROUP) % 4, row % GROUP
    half = row_x % 2

    def device(r, c):
        return {"row": r, "col": c}

    def peer(offset):
        dz, dx, dy = offset
        return (row_z + dz) % 2 * 16 + (row_x + dx) % 4 * GROUP + (lane + dy) % GROUP

    loads = [
        pltpu.make_async_copy(src, dst, load_sem.at[i])
        for i, (src, dst) in enumerate(
            [(feat_hbm, feat), (down_hbm, down), (dec_hbm, dec), (up_hbm, up)]
        )
    ]
    for load in loads:
        load.start()

    def weight_slot(owner_lane):
        start = pl.multiple_of(half * (GROUP * CIN) + owner_lane * CIN, CIN)
        return wg.at[:, pl.ds(start, CIN), :]

    def weight_piece(lane_to):
        return bott_hbm.at[:, :, pl.ds(pl.multiple_of(lane_to * 128, 128), 128)]

    own_weight = pltpu.make_async_copy(weight_piece(lane), weight_slot(lane), load_sem.at[4])
    own_weight.start()

    barrier = pltpu.get_barrier_semaphore()

    def greet(r, c):
        pl.semaphore_signal(barrier, inc=1, device_id=device(r, c), device_id_type=MESH)

    for offset in PEERS:
        greet(peer(offset), col)
    for dr in (-1, 0, 1):
        for dc in (-1, 1):
            greet((row + dr + ROWS) % ROWS, (col + dc + COLS) % COLS)

    rest = pl.multiple_of((1 - half) * (GROUP * CIN), GROUP * CIN)
    wg[:, pl.ds(rest, GROUP * CIN), :] = jnp.zeros((27, GROUP * CIN, 128), BF16)
    tiles[:, 0] = jnp.zeros((3, WB, 128), BF16)
    tiles[:, ROWS + 1] = jnp.zeros((3, WB, 128), BF16)

    for side, edge in ((0, row == 0), (1, row == ROWS - 1)):
        @pl.when(edge)
        def _():
            feat_in[side] = jnp.zeros((256, WIDTH), BF16)
            raised_in[side] = jnp.zeros((64, WIDTH), BF16)
            edges_in[:, side * (DEP + 1)] = jnp.zeros((2, C1, WIDTH), BF16)

    for side, edge in ((0, col == 0), (1, col == COLS - 1)):
        @pl.when(edge)
        def _():
            tiles[2 * side] = jnp.zeros((ROWS + 2, WB, 128), BF16)
            edges_in[side] = jnp.zeros((DEP + 2, C1, WIDTH), BF16)

    def inside(dr, dc):
        yes = None
        for at, step, count in ((row, dr, ROWS), (col, dc, COLS)):
            if step:
                here = at > 0 if step < 0 else at < count - 1
                yes = here if yes is None else jnp.logical_and(yes, here)
        return yes

    class Shift:
        def __init__(self, src, dst, send, recv, dr, dc):
            self.there, self.back = (dr, dc), (-dr, -dc)
            self.copy = pltpu.make_async_remote_copy(
                src_ref=src, dst_ref=dst, send_sem=send, recv_sem=recv,
                device_id=device((row + dr + ROWS) % ROWS, (col + dc + COLS) % COLS), device_id_type=MESH,
            )

        def start(self):
            @pl.when(inside(*self.there))
            def _():
                self.copy.start()

        def wait(self):
            @pl.when(inside(*self.there))
            def _():
                self.copy.wait_send()

            @pl.when(inside(*self.back))
            def _():
                self.copy.wait_recv()

    loads[0].wait()
    r_, c_ = iota((128, 256), 0), iota((128, 256), 1)
    pool_h = ones_where(((r_ % C1) == (c_ // HGT)) & ((r_ // C1) == (c_ % HGT) // 2))
    pool_h = jnp.concatenate([pool_h, pool_h], axis=1)
    r_, c_ = iota((64, WIDTH), 0), iota((64, WIDTH), 1)
    pool_w = jnp.where((c_ // 2) == (r_ % WB) * 4 + r_ // WB, 0.125, 0.0).astype(BF16)
    pooled = []
    for a in range(4):
        pair = feat[2 * a : 2 * a + 2].reshape(512, WIDTH)
        pooled.append(dot_nt(pool_w, dot(pool_h, pair).astype(BF16)).astype(BF16))
    pooled = jnp.concatenate(pooled, axis=1)

    loads[1].wait()
    total = jnp.zeros((WB, CB), F32)
    for c in range(4):
        total += dot(pooled[c * WB : (c + 1) * WB], down[:, c].reshape(512, CB))
    low = silu(total).astype(BF16)
    for k in range(4):
        lowered[k] = low[:, k * 128 : (k + 1) * 128]

    pl.semaphore_wait(barrier, ROWS - 1 + 6)

    for offset in PEERS:
        to = peer(offset)
        pltpu.make_async_remote_copy(
            src_ref=lowered.at[to // 8],
            dst_ref=tiles.at[1, 1 + row],
            send_sem=a_send,
            recv_sem=a_recv,
            device_id=device(to, col),
            device_id_type=MESH,
        ).start()

    weight_sends = []
    for j in range(1, GROUP):
        to = (lane + j) % GROUP
        copy = pltpu.make_async_remote_copy(
            src_ref=weight_piece(to),
            dst_ref=weight_slot(lane),
            send_sem=w_send.at[j - 1],
            recv_sem=w_recv.at[j - 1],
            device_id=device(row - lane + to, col),
            device_id_type=MESH,
        )
        copy.start()
        weight_sends.append(copy)

    feat_sends = [
        Shift(feat.at[0], feat_in.at[1], f_send.at[0], f_recv.at[0], -1, 0),
        Shift(feat.at[DEP - 1], feat_in.at[0], f_send.at[1], f_recv.at[1], 1, 0),
    ]
    for copy in feat_sends:
        copy.start()

    tiles[1, 1 + row] = lowered[row // 8]

    loads[2].wait()
    r_, c_ = iota((256, C1), 0), iota((256, C1), 1)
    spread_o = ones_where((r_ // HGT) == c_)
    r_, c_ = iota((C1, 256), 0), iota((C1, 256), 1)
    spread_c = ones_where((c_ // HGT) == r_)
    shift = (iota((256, 256), 1) % HGT) - (iota((256, 256), 0) % HGT)
    h_of = iota((256, C1), 0) % HGT
    for kd in range(3):
        for kw in range(3):
            total = jnp.zeros((256, 256), F32)
            sides = []
            for kh in range(3):
                taps = dot_nt(spread_o, dec[(kd * 3 + kh) * 3 + kw]).astype(BF16)
                total = jnp.where(shift == kh - 1, dot(taps, spread_c), total)
                if kh != 1:
                    edge = 0 if kh == 0 else HGT - 1
                    sides.append(jnp.where(h_of == edge, taps.astype(F32), 0.0))
            at = kd * 3 + kw
            band[:, at * 256 : (at + 1) * 256] = total.astype(BF16)
            band_h[:, at * 64 : (at + 1) * 64] = jnp.concatenate(sides, axis=1).astype(BF16)

    def all_tiles(ref, send, recv):
        span = ref.at[pl.ds(1, ROWS - 1)]
        return pltpu.make_async_remote_copy(
            src_ref=span, dst_ref=span, send_sem=send, recv_sem=recv,
            device_id=device(peer(PEERS[0]), col), device_id_type=MESH,
        )

    all_tiles(tiles.at[1], a_send, a_recv).wait_recv()

    halo_sends = []
    for i, (start, size) in enumerate((((1 - row_z) * 15, 17), (row_z * 17, 15))):
        span = pl.ds(1 + start, size)
        halo_sends.append(
            [
                Shift(tiles.at[1, span], tiles.at[1 - dc, span], h_send.at[i, s], h_recv.at[i, s], 0, dc)
                for s, dc in enumerate((-1, 1))
            ]
        )
    for pair in halo_sends:
        for copy in pair:
            copy.start()

    own_weight.wait()
    for copy in weight_sends:
        copy.wait()

    def patches(heights, start):
        return jnp.concatenate(
            [tiles[b, pl.ds(start + a, 16)].reshape(256, 128) for a in range(3) for b in heights], axis=1
        )

    def taps_of(heights):
        return jnp.concatenate(
            [
                jnp.concatenate([wg[a * 9 + b * 3 + c] for a in range(3) for b in heights], axis=0)
                for c in range(3)
            ],
            axis=1,
        )

    starts = ((1 - row_z) * 16, row_z * 16)
    inner_taps = taps_of((1,))
    inner = [dot(patches((1,), start), inner_taps) for start in starts]
    w_of = iota((256, 128), 0) % WB
    for dz, start in ((1, starts[0]), (0, starts[1])):
        for copy in halo_sends[1 - dz]:
            copy.wait()
        partial = inner[1 - dz] + dot(patches((0, 2), start), taps_of((0, 2)))
        before = pltpu.roll(partial[:, :128], 1, 0)
        after = pltpu.roll(partial[:, 256:], 255, 0)
        summed = partial[:, 128:256] + jnp.where(w_of == 0, 0.0, before) + jnp.where(w_of == WB - 1, 0.0, after)
        part[pl.ds(start, 16)] = summed.astype(BF16).reshape(16, WB, 128)
        for offset in PEERS:
            if offset[0] == dz:
                to = peer(offset)
                pltpu.make_async_remote_copy(
                    src_ref=part.at[to],
                    dst_ref=arrived.at[row],
                    send_sem=p_send,
                    recv_sem=p_recv,
                    device_id=device(to, col),
                    device_id_type=MESH,
                ).start()

    arrived[row] = part[row]
    r_, c_ = iota((512, WB), 0), iota((512, WB), 1)
    spread_w = ones_where((((r_ % WIDTH) // 8) == c_) & ((((r_ % WIDTH) // 2) % 4) == (r_ // WIDTH)))
    r_, c_ = iota((256, 128), 0), iota((256, 128), 1)
    raise_h = ones_where(((c_ % C1) == (r_ // HGT)) & ((c_ // C1) == (r_ % HGT) // 2))
    loads[3].wait()
    all_tiles(arrived, p_send, p_recv).wait_recv()

    groups = arrived[...].reshape(ROWS // GROUP, GROUP, WB, 128).astype(F32).sum(axis=0)
    middle = silu(jnp.concatenate([groups[k] for k in range(GROUP)], axis=1)).astype(BF16)
    spread = dot(spread_w, middle).astype(BF16)
    raised = jnp.zeros((512, WIDTH), F32)
    for c in range(4):
        raised += dot_nt(up[:, c].reshape(512, CB), spread[c * WIDTH : (c + 1) * WIDTH])

    odd = (iota((64, WIDTH), 1) % 2) == 1
    joined_sends = []
    for i, (first, dr) in enumerate(((0, -1), (384, 1))):
        raised_out[i] = jnp.where(odd, raised[first + 64 : first + 128], raised[first : first + 64]).astype(BF16)
        joined_sends.append(Shift(raised_out.at[i], raised_in.at[1 - i], j_send.at[i], j_recv.at[i], dr, 0))
        joined_sends[-1].start()
    raised = raised.astype(BF16)

    v_of = iota((256, WIDTH), 1)

    def shifted(value):
        v_ = v_of[: value.shape[0]]
        value = value.astype(F32)
        return (
            jnp.where(v_ == 0, 0.0, pltpu.roll(value, 1, 1)).astype(BF16),
            jnp.where(v_ == WIDTH - 1, 0.0, pltpu.roll(value, WIDTH - 1, 1)).astype(BF16),
        )

    r_, c_ = iota((64, 256), 0), iota((64, 256), 1)
    pick = ones_where(((c_ // HGT) == (r_ % C1)) & ((c_ % HGT) == (r_ // C1) * (HGT - 1)))
    lifts = [dot(raise_h, raised[a * 128 : (a + 1) * 128]) for a in range(4)]
    for d in (0, DEP - 1, *range(1, DEP - 1)):
        joined = (feat[d].astype(F32) + lifts[d // 2]).astype(BF16)
        slabs[1 + d, 1] = joined
        rim = dot(pick, joined).astype(BF16)
        edges_out[0, d] = rim[:C1]
        edges_out[1, d] = rim[C1:]
        if d in (0, DEP - 1):
            dr, slot = (-1, DEP + 1) if d == 0 else (1, 0)
            for side, dc in ((0, -1), (1, 1)):
                i = len(joined_sends)
                joined_sends.append(
                    Shift(edges_out.at[side, d], edges_in.at[1 - side, slot], j_send.at[i], j_recv.at[i], dr, dc)
                )
                joined_sends[-1].start()
    for side, dc in ((0, -1), (1, 1)):
        i = len(joined_sends)
        joined_sends.append(
            Shift(edges_out.at[side], edges_in.at[1 - side, pl.ds(1, DEP)], j_send.at[i], j_recv.at[i], 0, dc)
        )
        joined_sends[-1].start()

    for d in range(1, DEP + 1):
        slabs[d, 0], slabs[d, 2] = shifted(slabs[d, 1])
    for d in range(DEP):
        first, last = max(d, 1), min(d + 3, DEP + 1)
        accs[d] = dot(
            band[:, (first - d) * 768 : (last - d) * 768],
            slabs[first:last].reshape((last - first) * 768, WIDTH),
        )

    for copy in feat_sends + joined_sends:
        copy.wait()
    for side in range(2):
        both = raised_in[side].astype(F32)
        even_rows = jnp.where(odd, pltpu.roll(both, 1, 1), both)
        odd_rows = jnp.where(odd, both, pltpu.roll(both, WIDTH - 1, 1))
        lift = dot(raise_h, jnp.concatenate([even_rows, odd_rows], axis=0).astype(BF16))
        d = side * (DEP + 1)
        joined = (feat_in[side].astype(F32) + lift).astype(BF16)
        slabs[d, 1] = joined
        slabs[d, 0], slabs[d, 2] = shifted(joined)
    for d in range(DEP + 2):
        rim = jnp.concatenate([edges_in[0, d], edges_in[1, d]], axis=0)
        edges[d, 1] = rim
        edges[d, 0], edges[d, 2] = shifted(rim)
    for d in range(DEP):
        total = accs[d]
        if d == 0:
            total += dot(band[:, :768], slabs[0].reshape(768, WIDTH))
        if d == DEP - 1:
            total += dot(band[:, 1536:], slabs[DEP + 1].reshape(768, WIDTH))
        total += dot(band_h[...], edges[d : d + 3].reshape(9 * 64, WIDTH))
        out_ref[d] = silu(total).astype(BF16)

    all_tiles(tiles.at[1], a_send, a_recv).wait_send()
    all_tiles(arrived, p_send, p_recv).wait_send()


def body(features, down_weight, bott_weight, up_weight, dec_weight):
    dma = pltpu.SemaphoreType.DMA
    out = pl.pallas_call(
        kernel,
        out_shape=jax.ShapeDtypeStruct((DEP, 256, WIDTH), BF16),
        in_specs=[pl.BlockSpec(memory_space=pltpu.HBM)] * 5,
        out_specs=pl.BlockSpec(memory_space=pltpu.VMEM),
        scratch_shapes=[
            pltpu.VMEM((DEP, 256, WIDTH), BF16),
            pltpu.VMEM((16, 4, C1, CB), BF16),
            pltpu.VMEM((16, 4, C1, CB), BF16),
            pltpu.VMEM((27, C1, C1), BF16),
            pltpu.VMEM((27, 128, 128), BF16),
            pltpu.VMEM((4, WB, 128), BF16),
            pltpu.VMEM((3, ROWS + 2, WB, 128), BF16),
            pltpu.VMEM((ROWS, WB, 128), BF16),
            pltpu.VMEM((ROWS, WB, 128), BF16),
            pltpu.VMEM((256, 9 * 256), BF16),
            pltpu.VMEM((256, 9 * 64), BF16),
            pltpu.VMEM((DEP + 2, 3, 256, WIDTH), BF16),
            pltpu.VMEM((2, DEP, C1, WIDTH), BF16),
            pltpu.VMEM((2, DEP + 2, C1, WIDTH), BF16),
            pltpu.VMEM((DEP + 2, 3, 64, WIDTH), BF16),
            pltpu.VMEM((DEP, 256, WIDTH), F32),
            pltpu.VMEM((2, 256, WIDTH), BF16),
            pltpu.VMEM((2, 64, WIDTH), BF16),
            pltpu.VMEM((2, 64, WIDTH), BF16),
            dma((5,)), dma((3,)), dma((3,)), dma, dma, dma((2, 2)), dma((2, 2)), dma, dma, dma((8,)), dma((8,)),
            dma((2,)), dma((2,)),
        ],
        compiler_params=pltpu.CompilerParams(
            collective_id=0, has_side_effects=True, vmem_limit_bytes=60 * 1024 * 1024
        ),
        name="encode_decode",
    )(
        features.reshape(DEP, 256, WIDTH),
        down_weight.reshape(16, 4, C1, CB),
        bott_weight.reshape(27, CIN, CB),
        up_weight.reshape(16, 4, C1, CB),
        dec_weight.reshape(27, C1, C1),
    )
    return out.reshape(features.shape)


def solution(mesh):
    placed = (P("row", None, "col", None), P(), P(None, None, None, "row", None), P(), P())
    return jax.shard_map(
        body, mesh=mesh, in_specs=placed, out_specs=P("row", None, "col", None), check_vma=False
    )
```

```python
import jax
import jax.numpy as jnp
from jax import lax
from jax.experimental import pallas as pl
from jax.experimental.pallas import tpu as pltpu
from jax.sharding import PartitionSpec as P

MESH = pl.DeviceIdType.MESH
F32 = jnp.float32
BF16 = jnp.bfloat16
ROWS, COLS, GROUP = 32, 8, 4
C1, CB, WIDTH = 32, 512, 128
DEP, HGT, WB = 8, 8, 16
CIN = CB // ROWS
SEAM = ROWS // 2
NT = (((1,), (1,)), ((), ()))


def iota(shape, dim):
    return lax.broadcasted_iota(jnp.int32, shape, dim)


def ones_where(mask):
    return jnp.where(mask, 1.0, 0.0).astype(BF16)


def silu(v):
    return v / (1.0 + jnp.exp(-v))


def dot(a, b):
    return jnp.dot(a, b, preferred_element_type=F32)


def dot_nt(a, b):
    return lax.dot_general(a, b, NT, preferred_element_type=F32)


def hops(offset):
    dz, dx, dy = offset
    return 4 * dz + min(dx, 4 - dx) + min(dy, 4 - dy)


PEERS = sorted(
    [(dz, dx, dy) for dz in range(2) for dx in range(4) for dy in range(4) if dz + dx + dy],
    key=hops,
    reverse=True,
)


def kernel(
    feat_hbm, down_hbm, bott_hbm, up_hbm, dec_hbm, out_ref,
    feat, down, up, dec, wg, lowered, tiles, part, arrived, band, band_h,
    slabs, edges, accs, feat_in, feat_rim, feat_rim_in, beyond,
    raised_out, raised_in, rim_out, rim_in, corner_out, corner_in,
    load_sem, w_send, w_recv, a_send, a_recv, h_send, h_recv, p_send, p_recv, b_send, b_recv,
    j_send, j_recv, f_send, f_recv, s_send, s_recv,
):
    row, col = lax.axis_index("row"), lax.axis_index("col")
    row_z, row_x, lane = row // 16, (row // GROUP) % 4, row % GROUP
    half = row_x % 2

    def device(r, c):
        return {"row": r, "col": c}

    def peer(offset):
        dz, dx, dy = offset
        return (row_z + dz) % 2 * 16 + (row_x + dx) % 4 * GROUP + (lane + dy) % GROUP

    barrier = pltpu.get_barrier_semaphore()

    def greet(r, c):
        pl.semaphore_signal(barrier, inc=1, device_id=device(r, c), device_id_type=MESH)

    for offset in PEERS:
        greet(peer(offset), col)
    for dr in (-1, 0, 1):
        for dc in (-1, 1):
            greet((row + dr + ROWS) % ROWS, (col + dc + COLS) % COLS)

    loads = [
        pltpu.make_async_copy(src, dst, load_sem.at[i])
        for i, (src, dst) in enumerate(
            [(feat_hbm, feat), (down_hbm, down), (dec_hbm, dec), (up_hbm, up)]
        )
    ]
    for load in loads:
        load.start()

    def weight_slot(owner_lane):
        start = pl.multiple_of(half * (GROUP * CIN) + owner_lane * CIN, CIN)
        return wg.at[:, pl.ds(start, CIN), :]

    def weight_piece(lane_to):
        return bott_hbm.at[:, :, pl.ds(pl.multiple_of(lane_to * 128, 128), 128)]

    own_weight = pltpu.make_async_copy(weight_piece(lane), weight_slot(lane), load_sem.at[4])
    own_weight.start()

    rest = pl.multiple_of((1 - half) * (GROUP * CIN), GROUP * CIN)
    wg[:, pl.ds(rest, GROUP * CIN), :] = jnp.zeros((27, GROUP * CIN, 128), BF16)
    tiles[:, 0] = jnp.zeros((3, WB, 128), BF16)
    tiles[:, ROWS + 1] = jnp.zeros((3, WB, 128), BF16)

    for side, edge in ((0, row == 0), (1, row == ROWS - 1)):
        @pl.when(edge)
        def _():
            feat_in[side] = jnp.zeros((256, WIDTH), BF16)
            raised_in[side] = jnp.zeros((64, WIDTH), BF16)
            feat_rim_in[:, side * (DEP + 1)] = jnp.zeros((2, C1, WIDTH), BF16)
            corner_in[:, side] = jnp.zeros((2, C1, WIDTH), BF16)

    for side, edge in ((0, col == 0), (1, col == COLS - 1)):
        @pl.when(edge)
        def _():
            tiles[2 * side] = jnp.zeros((ROWS + 2, WB, 128), BF16)
            feat_rim_in[side] = jnp.zeros((DEP + 2, C1, WIDTH), BF16)
            rim_in[side] = jnp.zeros((64, WIDTH), BF16)
            corner_in[side] = jnp.zeros((2, C1, WIDTH), BF16)

    def inside(dr, dc):
        yes = None
        for at, step, count in ((row, dr, ROWS), (col, dc, COLS)):
            if step:
                here = at > 0 if step < 0 else at < count - 1
                yes = here if yes is None else jnp.logical_and(yes, here)
        return yes

    def off_seam(dr):
        return row != SEAM - 1 if dr > 0 else row != SEAM

    class Shift:
        def __init__(self, src, dst, send, recv, dr, dc, seam=None):
            self.there, self.back = inside(dr, dc), inside(-dr, -dc)
            if seam is not None:
                self.there = jnp.logical_and(self.there, off_seam(dr))
                self.back = jnp.logical_and(self.back, off_seam(-dr))
            self.copy = pltpu.make_async_remote_copy(
                src_ref=src, dst_ref=dst, send_sem=send, recv_sem=recv,
                device_id=device((row + dr + ROWS) % ROWS, (col + dc + COLS) % COLS), device_id_type=MESH,
            )

        def start(self):
            @pl.when(self.there)
            def _():
                self.copy.start()

        def wait(self):
            @pl.when(self.there)
            def _():
                self.copy.wait_send()

            @pl.when(self.back)
            def _():
                self.copy.wait_recv()

    loads[0].wait()
    r_, c_ = iota((128, 256), 0), iota((128, 256), 1)
    pool_h = ones_where(((r_ % C1) == (c_ // HGT)) & ((r_ // C1) == (c_ % HGT) // 2))
    pool_h = jnp.concatenate([pool_h, pool_h], axis=1)
    r_, c_ = iota((64, WIDTH), 0), iota((64, WIDTH), 1)
    pool_w = jnp.where((c_ // 2) == (r_ % WB) * 4 + r_ // WB, 0.125, 0.0).astype(BF16)
    pooled = []
    for a in range(4):
        pair = feat[2 * a : 2 * a + 2].reshape(512, WIDTH)
        pooled.append(dot_nt(pool_w, dot(pool_h, pair).astype(BF16)).astype(BF16))
    pooled = jnp.concatenate(pooled, axis=1)

    loads[1].wait()
    total = jnp.zeros((WB, CB), F32)
    for c in range(4):
        total += dot(pooled[c * WB : (c + 1) * WB], down[:, c].reshape(512, CB))
    low = silu(total).astype(BF16)
    for k in range(4):
        lowered[k] = low[:, k * 128 : (k + 1) * 128]

    r_, c_ = iota((64, 256), 0), iota((64, 256), 1)
    pick = ones_where(((c_ // HGT) == (r_ % C1)) & ((c_ % HGT) == (r_ // C1) * (HGT - 1)))
    for d in range(DEP):
        rim = dot(pick, feat[d]).astype(BF16)
        feat_rim[0, d] = rim[:C1]
        feat_rim[1, d] = rim[C1:]

    pl.semaphore_wait(barrier, ROWS - 1 + 6)

    for offset in PEERS:
        to = peer(offset)
        pltpu.make_async_remote_copy(
            src_ref=lowered.at[to // 8],
            dst_ref=tiles.at[1, 1 + row],
            send_sem=a_send,
            recv_sem=a_recv,
            device_id=device(to, col),
            device_id_type=MESH,
        ).start()

    weight_sends = []
    for j in range(1, GROUP):
        to = (lane + j) % GROUP
        copy = pltpu.make_async_remote_copy(
            src_ref=weight_piece(to),
            dst_ref=weight_slot(lane),
            send_sem=w_send.at[j - 1],
            recv_sem=w_recv.at[j - 1],
            device_id=device(row - lane + to, col),
            device_id_type=MESH,
        )
        copy.start()
        weight_sends.append(copy)

    sides, ends = ((0, -1), (1, 1)), ((0, -1, 0), (1, 1, DEP - 1))
    feat_moves = [(feat.at[d], feat_in.at[1 - e], dr, 0) for e, dr, d in ends]
    feat_moves += [(feat_rim.at[s], feat_rim_in.at[1 - s, pl.ds(1, DEP)], 0, dc) for s, dc in sides]
    feat_moves += [
        (feat_rim.at[s, d], feat_rim_in.at[1 - s, (1 - e) * (DEP + 1)], dr, dc) for s, dc in sides for e, dr, d in ends
    ]
    feat_sends = [
        Shift(src, dst, f_send.at[i], f_recv.at[i], dr, dc) for i, (src, dst, dr, dc) in enumerate(feat_moves)
    ]
    for copy in feat_sends:
        copy.start()

    tiles[1, 1 + row] = lowered[row // 8]

    loads[2].wait()
    r_, c_ = iota((256, C1), 0), iota((256, C1), 1)
    spread_o = ones_where((r_ // HGT) == c_)
    r_, c_ = iota((C1, 256), 0), iota((C1, 256), 1)
    spread_c = ones_where((c_ // HGT) == r_)
    shift = (iota((256, 256), 1) % HGT) - (iota((256, 256), 0) % HGT)
    h_of = iota((256, C1), 0) % HGT
    for kd in range(3):
        for kw in range(3):
            total = jnp.zeros((256, 256), F32)
            tops = []
            for kh in range(3):
                taps = dot_nt(spread_o, dec[(kd * 3 + kh) * 3 + kw]).astype(BF16)
                total = jnp.where(shift == kh - 1, dot(taps, spread_c), total)
                if kh != 1:
                    edge = 0 if kh == 0 else HGT - 1
                    tops.append(jnp.where(h_of == edge, taps.astype(F32), 0.0))
            at = kd * 3 + kw
            band[:, at * 256 : (at + 1) * 256] = total.astype(BF16)
            band_h[:, at * 64 : (at + 1) * 64] = jnp.concatenate(tops, axis=1).astype(BF16)

    def all_tiles(ref, send, recv):
        span = ref.at[pl.ds(1, ROWS - 1)]
        return pltpu.make_async_remote_copy(
            src_ref=span, dst_ref=span, send_sem=send, recv_sem=recv,
            device_id=device(peer(PEERS[0]), col), device_id_type=MESH,
        )

    all_tiles(tiles.at[1], a_send, a_recv).wait_recv()

    halo_sends = []
    for i, (start, size) in enumerate((((1 - row_z) * 15, 17), (row_z * 17, 15))):
        span = pl.ds(1 + start, size)
        halo_sends.append(
            [
                Shift(tiles.at[1, span], tiles.at[1 - dc, span], h_send.at[i, s], h_recv.at[i, s], 0, dc)
                for s, dc in enumerate((-1, 1))
            ]
        )
    for pair in halo_sends:
        for copy in pair:
            copy.start()

    own_weight.wait()
    for copy in weight_sends:
        copy.wait()

    def patches(heights, start):
        return jnp.concatenate(
            [tiles[b, pl.ds(start + a, 16)].reshape(256, 128) for a in range(3) for b in heights], axis=1
        )

    def taps_of(heights):
        return jnp.concatenate(
            [
                jnp.concatenate([wg[a * 9 + b * 3 + c] for a in range(3) for b in heights], axis=0)
                for c in range(3)
            ],
            axis=1,
        )

    def beyond_copy(i, to):
        return pltpu.make_async_remote_copy(
            src_ref=part.at[2 * SEAM - 1 - to], dst_ref=beyond.at[row],
            send_sem=b_send.at[i], recv_sem=b_recv, device_id=device(to, col), device_id_type=MESH,
        )

    starts = ((1 - row_z) * 16, row_z * 16)
    inner_taps = taps_of((1,))
    inner = [dot(patches((1,), start), inner_taps) for start in starts]
    w_of = iota((256, 128), 0) % WB
    for dz, start in ((1, starts[0]), (0, starts[1])):
        for copy in halo_sends[1 - dz]:
            copy.wait()
        partial = inner[1 - dz] + dot(patches((0, 2), start), taps_of((0, 2)))
        before = pltpu.roll(partial[:, :128], 1, 0)
        after = pltpu.roll(partial[:, 256:], 255, 0)
        summed = partial[:, 128:256] + jnp.where(w_of == 0, 0.0, before) + jnp.where(w_of == WB - 1, 0.0, after)
        part[pl.ds(start, 16)] = summed.astype(BF16).reshape(16, WB, 128)
        if dz == 0:
            for i, to in enumerate((SEAM, SEAM - 1)):
                @pl.when(row != to)
                def _():
                    beyond_copy(i, to).start()

                @pl.when(row == to)
                def _():
                    beyond[row] = part[2 * SEAM - 1 - to]

        for offset in PEERS:
            if offset[0] == dz:
                to = peer(offset)
                pltpu.make_async_remote_copy(
                    src_ref=part.at[to],
                    dst_ref=arrived.at[row],
                    send_sem=p_send,
                    recv_sem=p_recv,
                    device_id=device(to, col),
                    device_id_type=MESH,
                ).start()

    arrived[row] = part[row]
    r_, c_ = iota((512, WB), 0), iota((512, WB), 1)
    spread_w = ones_where((((r_ % WIDTH) // 8) == c_) & ((((r_ % WIDTH) // 2) % 4) == (r_ // WIDTH)))
    r_, c_ = iota((256, 128), 0), iota((256, 128), 1)
    raise_h = ones_where(((c_ % C1) == (r_ // HGT)) & ((c_ // C1) == (r_ % HGT) // 2))
    loads[3].wait()
    all_tiles(arrived, p_send, p_recv).wait_recv()

    def spread_of(shares):
        groups = shares.reshape(ROWS // GROUP, GROUP, WB, 128).astype(F32).sum(axis=0)
        middle = silu(jnp.concatenate([groups[k] for k in range(GROUP)], axis=1)).astype(BF16)
        return dot(spread_w, middle).astype(BF16)

    def raised_layer(a, spread):
        total = jnp.zeros((128, WIDTH), F32)
        for c in range(4):
            total += dot_nt(up[pl.ds(a * 4, 4), c].reshape(128, CB), spread[c * WIDTH : (c + 1) * WIDTH])
        return total

    odd = (iota((64, WIDTH), 1) % 2) == 1

    def packed(value):
        return jnp.where(odd, value[64:], value[:64]).astype(BF16)

    def unpacked(value):
        both = value.astype(F32)
        even_rows = jnp.where(odd, pltpu.roll(both, 1, 1), both)
        odd_rows = jnp.where(odd, both, pltpu.roll(both, WIDTH - 1, 1))
        return jnp.concatenate([even_rows, odd_rows], axis=0)

    spread = spread_of(arrived[...])
    raised = [None] * 4
    joined_sends = []

    def send(src, dst, dr, dc, seam=None):
        i = len(joined_sends)
        joined_sends.append(Shift(src, dst, j_send.at[i], j_recv.at[i], dr, dc, seam))
        joined_sends[-1].start()

    for e, dr, a in ((0, -1, 0), (1, 1, 3)):
        raised[a] = raised_layer(a, spread)
        raised_out[e] = packed(raised[a])
        send(raised_out.at[e], raised_in.at[1 - e], dr, 0, False)
        for s, dc in sides:
            corner_out[s, e] = raised[a][96 * s : 96 * s + C1].astype(BF16)
            send(corner_out.at[s, e], corner_in.at[1 - s, 1 - e], dr, dc, False)
    for a in (1, 2):
        raised[a] = raised_layer(a, spread)
    for s, dc in sides:
        rim_out[s] = packed(jnp.concatenate([raised[a][96 * s : 96 * s + C1] for a in range(4)], axis=0))
        send(rim_out.at[s], rim_in.at[1 - s], 0, dc)

    for copy in feat_sends:
        copy.wait()

    for e, here, dr in ((0, SEAM, -1), (1, SEAM - 1, 1)):
        @pl.when(row == here)
        def _():
            all_tiles(beyond, b_send.at[0], b_recv).wait_recv()
            layer = raised_layer(3 * (1 - e), spread_of(beyond[...]))
            raised_in[e] = packed(layer)
            for s in range(2):
                corner_out[s, 2 + e] = layer[96 * s : 96 * s + C1].astype(BF16)

    for e, here in ((0, SEAM), (1, SEAM - 1)):
        for s, dc in sides:
            copy = Shift(
                corner_out.at[s, 2 + e], corner_in.at[1 - s, e], s_send.at[s, e], s_recv.at[s, e], 0, dc
            )
            copy.there = jnp.logical_and(copy.there, row == here)
            copy.back = jnp.logical_and(copy.back, row == here)
            copy.start()
            joined_sends.append(copy)

    v_of = iota((256, WIDTH), 1)

    def shifted(value):
        v_ = v_of[: value.shape[0]]
        value = value.astype(F32)
        return (
            jnp.where(v_ == 0, 0.0, pltpu.roll(value, 1, 1)).astype(BF16),
            jnp.where(v_ == WIDTH - 1, 0.0, pltpu.roll(value, WIDTH - 1, 1)).astype(BF16),
        )

    def store_slab(i, layer, lift):
        joined = layer.astype(F32) + lift
        slabs[i, 1] = joined.astype(BF16)
        slabs[i, 0], slabs[i, 2] = shifted(joined.astype(BF16))

    for d in range(DEP):
        if d % 2 == 0:
            lift = dot(raise_h, raised[d // 2].astype(BF16))
        store_slab(1 + d, feat[d], lift)

    def windows(ref, d, first, last, size):
        return jnp.concatenate(
            [ref[d + i + first : d + i + last].reshape((last - first) * 3 * size, WIDTH) for i in range(2)], axis=1
        )

    spans = ((1, 3), (0, 3), (0, 3), (0, 2))
    for p, (first, last) in enumerate(spans):
        accs[p] = dot(band[:, first * 768 : last * 768], windows(slabs, 2 * p, first, last, 256))

    for copy in joined_sends:
        copy.wait()
    for e in range(2):
        store_slab(e * (DEP + 1), feat_in[e], dot(raise_h, unpacked(raised_in[e]).astype(BF16)))
    rims = [unpacked(rim_in[s]) for s in range(2)]
    for d in range(DEP + 2):
        rim = []
        for s in range(2):
            if d in (0, DEP + 1):
                lift = corner_in[s, d // (DEP + 1)].astype(F32)
            else:
                a = (d - 1) // 2
                lift = rims[s][a * C1 : (a + 1) * C1]
            rim.append((feat_rim_in[s, d].astype(F32) + lift).astype(BF16))
        rim = jnp.concatenate(rim, axis=0)
        edges[d, 1] = rim
        edges[d, 0], edges[d, 2] = shifted(rim)
    for p in range(4):
        total = accs[p] + dot(band_h[...], windows(edges, 2 * p, 0, 3, 64))
        if p == 0:
            total += dot(band[:, :768], windows(slabs, 0, 0, 1, 256))
        if p == 3:
            total += dot(band[:, 1536:], windows(slabs, 6, 2, 3, 256))
        total = silu(total).astype(BF16)
        out_ref[2 * p] = total[:, :WIDTH]
        out_ref[2 * p + 1] = total[:, WIDTH:]

    all_tiles(tiles.at[1], a_send, a_recv).wait_send()
    all_tiles(arrived, p_send, p_recv).wait_send()
    for i, to in enumerate((SEAM, SEAM - 1)):
        @pl.when(row != to)
        def _():
            beyond_copy(i, to).wait_send()


def body(features, down_weight, bott_weight, up_weight, dec_weight):
    dma = pltpu.SemaphoreType.DMA
    out = pl.pallas_call(
        kernel,
        out_shape=jax.ShapeDtypeStruct((DEP, 256, WIDTH), BF16),
        in_specs=[pl.BlockSpec(memory_space=pltpu.HBM)] * 5,
        out_specs=pl.BlockSpec(memory_space=pltpu.VMEM),
        scratch_shapes=[
            pltpu.VMEM((DEP, 256, WIDTH), BF16),
            pltpu.VMEM((16, 4, C1, CB), BF16),
            pltpu.VMEM((16, 4, C1, CB), BF16),
            pltpu.VMEM((27, C1, C1), BF16),
            pltpu.VMEM((27, 128, 128), BF16),
            pltpu.VMEM((4, WB, 128), BF16),
            pltpu.VMEM((3, ROWS + 2, WB, 128), BF16),
            pltpu.VMEM((ROWS, WB, 128), BF16),
            pltpu.VMEM((ROWS, WB, 128), BF16),
            pltpu.VMEM((256, 9 * 256), BF16),
            pltpu.VMEM((256, 9 * 64), BF16),
            pltpu.VMEM((DEP + 2, 3, 256, WIDTH), BF16),
            pltpu.VMEM((DEP + 2, 3, 64, WIDTH), BF16),
            pltpu.VMEM((DEP // 2, 256, 2 * WIDTH), F32),
            pltpu.VMEM((2, 256, WIDTH), BF16),
            pltpu.VMEM((2, DEP, C1, WIDTH), BF16),
            pltpu.VMEM((2, DEP + 2, C1, WIDTH), BF16),
            pltpu.VMEM((ROWS, WB, 128), BF16),
            pltpu.VMEM((2, 64, WIDTH), BF16),
            pltpu.VMEM((2, 64, WIDTH), BF16),
            pltpu.VMEM((2, 64, WIDTH), BF16),
            pltpu.VMEM((2, 64, WIDTH), BF16),
            pltpu.VMEM((2, 4, C1, WIDTH), BF16),
            pltpu.VMEM((2, 2, C1, WIDTH), BF16),
            dma((5,)), dma((3,)), dma((3,)), dma, dma, dma((2, 2)), dma((2, 2)), dma, dma, dma((2,)), dma,
            dma((8,)), dma((8,)), dma((8,)), dma((8,)), dma((2, 2)), dma((2, 2)),
        ],
        compiler_params=pltpu.CompilerParams(
            collective_id=0, has_side_effects=True, vmem_limit_bytes=60 * 1024 * 1024
        ),
        name="encode_decode",
    )(
        features.reshape(DEP, 256, WIDTH),
        down_weight.reshape(16, 4, C1, CB),
        bott_weight.reshape(27, CIN, CB),
        up_weight.reshape(16, 4, C1, CB),
        dec_weight.reshape(27, C1, C1),
    )
    return out.reshape(features.shape)


def solution(mesh):
    placed = (P("row", None, "col", None), P(), P(None, None, None, "row", None), P(), P())
    return jax.shard_map(
        body, mesh=mesh, in_specs=placed, out_specs=P("row", None, "col", None), check_vma=False
    )
```

```python
import jax
import jax.numpy as jnp
from jax import lax
from jax.experimental import pallas as pl
from jax.experimental.pallas import tpu as pltpu
from jax.sharding import PartitionSpec as P

MESH = pl.DeviceIdType.MESH
F32 = jnp.float32
BF16 = jnp.bfloat16
ROWS, COLS, GROUP = 32, 8, 4
C1, CB, WIDTH = 32, 512, 128
DEP, HGT, WB = 8, 8, 16
CIN = CB // ROWS
SEAM = ROWS // 2
NT = (((1,), (1,)), ((), ()))


def iota(shape, dim):
    return lax.broadcasted_iota(jnp.int32, shape, dim)


def ones_where(mask):
    return jnp.where(mask, 1.0, 0.0).astype(BF16)


def silu(v):
    return 0.5 * v * (1.0 + jnp.tanh(0.5 * v))


def dot(a, b):
    return jnp.dot(a, b, preferred_element_type=F32)


def dot_nt(a, b):
    return lax.dot_general(a, b, NT, preferred_element_type=F32)


def hops(offset):
    dz, dx, dy = offset
    return 4 * dz + min(dx, 4 - dx) + min(dy, 4 - dy)


PEERS = sorted(
    [(dz, dx, dy) for dz in range(2) for dx in range(4) for dy in range(4) if dz + dx + dy],
    key=hops,
    reverse=True,
)


def kernel(
    feat_hbm, down_hbm, bott_hbm, up_hbm, dec_hbm, out_ref,
    feat, down, up, dec, wg, lowered, tiles, part, arrived, band, band_h,
    slabs, edges, accs, feat_in, feat_rim, feat_rim_in, beyond,
    raised_out, raised_in, rim_out, rim_in, corner_out, corner_in,
    load_sem, w_send, w_recv, a_send, a_recv, h_send, h_recv, p_send, p_recv, b_send, b_recv,
    j_send, j_recv, f_send, f_recv, s_send, s_recv,
):
    row, col = lax.axis_index("row"), lax.axis_index("col")
    row_z, row_x, lane = row // 16, (row // GROUP) % 4, row % GROUP
    half = row_x % 2

    def device(r, c):
        return {"row": r, "col": c}

    def peer(offset):
        dz, dx, dy = offset
        return (row_z + dz) % 2 * 16 + (row_x + dx) % 4 * GROUP + (lane + dy) % GROUP

    barrier = pltpu.get_barrier_semaphore()

    def greet(r, c):
        pl.semaphore_signal(barrier, inc=1, device_id=device(r, c), device_id_type=MESH)

    for offset in PEERS:
        greet(peer(offset), col)
    for dr in (-1, 0, 1):
        for dc in (-1, 1):
            greet((row + dr + ROWS) % ROWS, (col + dc + COLS) % COLS)

    loads = [
        pltpu.make_async_copy(src, dst, load_sem.at[i])
        for i, (src, dst) in enumerate(
            [(feat_hbm, feat), (down_hbm, down), (dec_hbm, dec), (up_hbm, up)]
        )
    ]
    for load in loads:
        load.start()

    def weight_slot(owner_lane):
        start = pl.multiple_of(half * (GROUP * CIN) + owner_lane * CIN, CIN)
        return wg.at[:, pl.ds(start, CIN), :]

    def weight_piece(lane_to):
        return bott_hbm.at[:, :, pl.ds(pl.multiple_of(lane_to * 128, 128), 128)]

    own_weight = pltpu.make_async_copy(weight_piece(lane), weight_slot(lane), load_sem.at[4])
    own_weight.start()

    rest = pl.multiple_of((1 - half) * (GROUP * CIN), GROUP * CIN)
    wg[:, pl.ds(rest, GROUP * CIN), :] = jnp.zeros((27, GROUP * CIN, 128), BF16)
    tiles[:, 0] = jnp.zeros((3, WB, 128), BF16)
    tiles[:, ROWS + 1] = jnp.zeros((3, WB, 128), BF16)

    for side, edge in ((0, row == 0), (1, row == ROWS - 1)):
        @pl.when(edge)
        def _():
            feat_in[side] = jnp.zeros((256, WIDTH), BF16)
            raised_in[side] = jnp.zeros((64, WIDTH), BF16)
            feat_rim_in[:, side * (DEP + 1)] = jnp.zeros((2, C1, WIDTH), BF16)
            corner_in[:, side] = jnp.zeros((2, C1, WIDTH), BF16)

    for side, edge in ((0, col == 0), (1, col == COLS - 1)):
        @pl.when(edge)
        def _():
            tiles[2 * side] = jnp.zeros((ROWS + 2, WB, 128), BF16)
            feat_rim_in[side] = jnp.zeros((DEP + 2, C1, WIDTH), BF16)
            rim_in[side] = jnp.zeros((64, WIDTH), BF16)
            corner_in[side] = jnp.zeros((2, C1, WIDTH), BF16)

    def inside(dr, dc):
        yes = None
        for at, step, count in ((row, dr, ROWS), (col, dc, COLS)):
            if step:
                here = at > 0 if step < 0 else at < count - 1
                yes = here if yes is None else jnp.logical_and(yes, here)
        return yes

    def off_seam(dr):
        return row != SEAM - 1 if dr > 0 else row != SEAM

    class Shift:
        def __init__(self, src, dst, send, recv, dr, dc, seam=None):
            self.there, self.back = inside(dr, dc), inside(-dr, -dc)
            if seam is not None:
                self.there = jnp.logical_and(self.there, off_seam(dr))
                self.back = jnp.logical_and(self.back, off_seam(-dr))
            self.copy = pltpu.make_async_remote_copy(
                src_ref=src, dst_ref=dst, send_sem=send, recv_sem=recv,
                device_id=device((row + dr + ROWS) % ROWS, (col + dc + COLS) % COLS), device_id_type=MESH,
            )

        def start(self, also=None):
            @pl.when(self.there if also is None else jnp.logical_and(self.there, also))
            def _():
                self.copy.start()

        def wait(self):
            @pl.when(self.there)
            def _():
                self.copy.wait_send()

            @pl.when(self.back)
            def _():
                self.copy.wait_recv()

    loads[0].wait()
    r_, c_ = iota((128, 256), 0), iota((128, 256), 1)
    pool_h = ones_where(((r_ % C1) == (c_ // HGT)) & ((r_ // C1) == (c_ % HGT) // 2))
    pool_h = jnp.concatenate([pool_h, pool_h], axis=1)
    r_, c_ = iota((64, WIDTH), 0), iota((64, WIDTH), 1)
    pool_w = jnp.where((c_ // 2) == (r_ % WB) * 4 + r_ // WB, 0.125, 0.0).astype(BF16)
    pooled = []
    for a in range(4):
        pair = feat[2 * a : 2 * a + 2].reshape(512, WIDTH)
        pooled.append(dot_nt(pool_w, dot(pool_h, pair).astype(BF16)).astype(BF16))
    pooled = jnp.concatenate(pooled, axis=1)

    loads[1].wait()
    total = jnp.zeros((WB, CB), F32)
    for c in range(4):
        total += dot(pooled[c * WB : (c + 1) * WB], down[:, c].reshape(512, CB))
    low = silu(total).astype(BF16)
    for k in range(4):
        lowered[k] = low[:, k * 128 : (k + 1) * 128]

    r_, c_ = iota((64, 256), 0), iota((64, 256), 1)
    pick = ones_where(((c_ // HGT) == (r_ % C1)) & ((c_ % HGT) == (r_ // C1) * (HGT - 1)))
    for d in range(DEP):
        rim = dot(pick, feat[d]).astype(BF16)
        feat_rim[0, d] = rim[:C1]
        feat_rim[1, d] = rim[C1:]

    pl.semaphore_wait(barrier, ROWS - 1 + 6)

    for offset in PEERS:
        to = peer(offset)
        pltpu.make_async_remote_copy(
            src_ref=lowered.at[to // 8],
            dst_ref=tiles.at[1, 1 + row],
            send_sem=a_send,
            recv_sem=a_recv,
            device_id=device(to, col),
            device_id_type=MESH,
        ).start()

    core = col % 2

    def taps_at(ref, start, size):
        return ref.at[pl.ds(start, size)]

    weight_sends = []
    for j in range(1, GROUP):
        to = (lane + j) % GROUP
        copy = pltpu.make_async_remote_copy(
            src_ref=taps_at(weight_piece(to), core * 13, 14),
            dst_ref=taps_at(weight_slot(lane), core * 13, 14),
            send_sem=w_send.at[j - 1],
            recv_sem=w_recv.at[j - 1],
            device_id=device(row - lane + to, col),
            device_id_type=MESH,
        )
        copy.start()
        weight_sends.append(copy)
    twin_sends = []
    for j in range(1, GROUP):
        slot = taps_at(weight_slot((lane + j) % GROUP), core * 14, 13)
        twin_sends.append(
            pltpu.make_async_remote_copy(
                src_ref=slot, dst_ref=slot, send_sem=w_send.at[GROUP + j - 2], recv_sem=w_recv.at[GROUP + j - 2],
                device_id=device(row, col + 1 - 2 * core), device_id_type=MESH,
            )
        )

    sides, ends = ((0, -1), (1, 1)), ((0, -1, 0), (1, 1, DEP - 1))
    feat_moves = [(feat.at[d], feat_in.at[1 - e], dr, 0) for e, dr, d in ends]
    feat_moves += [(feat_rim.at[s], feat_rim_in.at[1 - s, pl.ds(1, DEP)], 0, dc) for s, dc in sides]
    feat_moves += [
        (feat_rim.at[s, d], feat_rim_in.at[1 - s, (1 - e) * (DEP + 1)], dr, dc) for s, dc in sides for e, dr, d in ends
    ]
    feat_sends = [
        Shift(src, dst, f_send.at[i], f_recv.at[i], dr, dc) for i, (src, dst, dr, dc) in enumerate(feat_moves)
    ]
    for copy, (_, _, dr, _) in zip(feat_sends, feat_moves):
        if dr:
            copy.start(jnp.logical_not(off_seam(dr)))

    tiles[1, 1 + row] = lowered[row // 8]

    loads[2].wait()
    r_, c_ = iota((256, C1), 0), iota((256, C1), 1)
    spread_o = ones_where((r_ // HGT) == c_)
    r_, c_ = iota((C1, 256), 0), iota((C1, 256), 1)
    spread_c = ones_where((c_ // HGT) == r_)
    shift = (iota((256, 256), 1) % HGT) - (iota((256, 256), 0) % HGT)
    h_of = iota((256, C1), 0) % HGT
    for kd in range(3):
        for kw in range(3):
            total = jnp.zeros((256, 256), F32)
            tops = []
            for kh in range(3):
                taps = dot_nt(spread_o, dec[(kd * 3 + kh) * 3 + kw]).astype(BF16)
                total = jnp.where(shift == kh - 1, dot(taps, spread_c), total)
                if kh != 1:
                    edge = 0 if kh == 0 else HGT - 1
                    tops.append(jnp.where(h_of == edge, taps.astype(F32), 0.0))
            at = kd * 3 + kw
            band[:, at * 256 : (at + 1) * 256] = total.astype(BF16)
            band_h[:, at * 64 : (at + 1) * 64] = jnp.concatenate(tops, axis=1).astype(BF16)

    def all_tiles(ref, send, recv):
        span = ref.at[pl.ds(1, ROWS - 1)]
        return pltpu.make_async_remote_copy(
            src_ref=span, dst_ref=span, send_sem=send, recv_sem=recv,
            device_id=device(peer(PEERS[0]), col), device_id_type=MESH,
        )

    all_tiles(tiles.at[1], a_send, a_recv).wait_recv()

    halo_sends = []
    for i, (start, size) in enumerate((((1 - row_z) * 15, 17), (row_z * 17, 15))):
        span = pl.ds(1 + start, size)
        halo_sends.append(
            [
                Shift(tiles.at[1, span], tiles.at[1 - dc, span], h_send.at[i, s], h_recv.at[i, s], 0, dc)
                for s, dc in enumerate((-1, 1))
            ]
        )
    for pair in halo_sends:
        for copy in pair:
            copy.start()

    own_weight.wait()
    for copy in weight_sends:
        copy.wait()
    for copy in twin_sends:
        copy.start()
    for copy, (_, _, dr, _) in zip(feat_sends, feat_moves):
        copy.start(off_seam(dr) if dr else None)
    for copy in twin_sends:
        copy.wait()

    def patches(heights, start):
        return jnp.concatenate(
            [tiles[b, pl.ds(start + a, 16)].reshape(256, 128) for a in range(3) for b in heights], axis=1
        )

    def taps_of(heights):
        return jnp.concatenate(
            [
                jnp.concatenate([wg[a * 9 + b * 3 + c] for a in range(3) for b in heights], axis=0)
                for c in range(3)
            ],
            axis=1,
        )

    def beyond_copy(i, to):
        return pltpu.make_async_remote_copy(
            src_ref=part.at[2 * SEAM - 1 - to], dst_ref=beyond.at[row],
            send_sem=b_send.at[i], recv_sem=b_recv, device_id=device(to, col), device_id_type=MESH,
        )

    starts = ((1 - row_z) * 16, row_z * 16)
    inner_taps = taps_of((1,))
    inner = [dot(patches((1,), start), inner_taps) for start in starts]
    w_of = iota((256, 128), 0) % WB
    for dz, start in ((1, starts[0]), (0, starts[1])):
        for copy in halo_sends[1 - dz]:
            copy.wait()
        partial = inner[1 - dz] + dot(patches((0, 2), start), taps_of((0, 2)))
        before = pltpu.roll(partial[:, :128], 1, 0)
        after = pltpu.roll(partial[:, 256:], 255, 0)
        summed = partial[:, 128:256] + jnp.where(w_of == 0, 0.0, before) + jnp.where(w_of == WB - 1, 0.0, after)
        part[pl.ds(start, 16)] = summed.astype(BF16).reshape(16, WB, 128)
        if dz == 0:
            for i, to in enumerate((SEAM, SEAM - 1)):
                @pl.when(row != to)
                def _():
                    beyond_copy(i, to).start()

                @pl.when(row == to)
                def _():
                    beyond[row] = part[2 * SEAM - 1 - to]

        for offset in PEERS:
            if offset[0] == dz:
                to = peer(offset)
                pltpu.make_async_remote_copy(
                    src_ref=part.at[to],
                    dst_ref=arrived.at[row],
                    send_sem=p_send,
                    recv_sem=p_recv,
                    device_id=device(to, col),
                    device_id_type=MESH,
                ).start()

    arrived[row] = part[row]
    r_, c_ = iota((WB, 512), 1), iota((WB, 512), 0)
    spread_w = ones_where((((r_ % WIDTH) // 8) == c_) & ((((r_ % WIDTH) // 2) % 4) == (r_ // WIDTH)))
    r_, c_ = iota((256, 128), 0), iota((256, 128), 1)
    raise_h = ones_where(((c_ % C1) == (r_ // HGT)) & ((c_ // C1) == (r_ % HGT) // 2))
    loads[3].wait()
    all_tiles(arrived, p_send, p_recv).wait_recv()

    def spread_of(shares):
        groups = shares.reshape(ROWS // GROUP, GROUP, WB, 128).astype(F32).sum(axis=0)
        middle = silu(jnp.concatenate([groups[k] for k in range(GROUP)], axis=1)).astype(BF16)
        across = lax.dot_general(middle, spread_w, (((0,), (0,)), ((), ())), preferred_element_type=F32)
        across = across.astype(BF16)
        return jnp.concatenate([across[:, c * WIDTH : (c + 1) * WIDTH] for c in range(4)], axis=0)

    def raised_layers(layers, spread):
        rows = [
            jnp.concatenate([up[a * 4 : a * 4 + 4, c].reshape(128, CB) for a in layers], axis=0) for c in range(4)
        ]
        return dot(jnp.concatenate(rows, axis=1), spread)

    odd = (iota((64, WIDTH), 1) % 2) == 1

    def packed(value):
        return jnp.where(odd, value[64:], value[:64]).astype(BF16)

    def unpacked(value):
        both = value.astype(F32)
        even_rows = jnp.where(odd, pltpu.roll(both, 1, 1), both)
        odd_rows = jnp.where(odd, both, pltpu.roll(both, WIDTH - 1, 1))
        return jnp.concatenate([even_rows, odd_rows], axis=0)

    spread = spread_of(arrived[...])
    raised = [None] * 4
    joined_sends = []

    def send(src, dst, dr, dc, seam=None):
        i = len(joined_sends)
        joined_sends.append(Shift(src, dst, j_send.at[i], j_recv.at[i], dr, dc, seam))
        joined_sends[-1].start()

    outer = raised_layers((0, 3), spread)
    raised[0], raised[3] = outer[:128], outer[128:]
    for e, dr, a in ((0, -1, 0), (1, 1, 3)):
        raised_out[e] = packed(raised[a])
        send(raised_out.at[e], raised_in.at[1 - e], dr, 0, False)
        for s, dc in sides:
            corner_out[s, e] = raised[a][96 * s : 96 * s + C1].astype(BF16)
            send(corner_out.at[s, e], corner_in.at[1 - s, 1 - e], dr, dc, False)
    inner = raised_layers((1, 2), spread)
    raised[1], raised[2] = inner[:128], inner[128:]
    for s, dc in sides:
        rim_out[s] = packed(jnp.concatenate([raised[a][96 * s : 96 * s + C1] for a in range(4)], axis=0))
        send(rim_out.at[s], rim_in.at[1 - s], 0, dc)

    for copy in feat_sends:
        copy.wait()

    for e, here, dr in ((0, SEAM, -1), (1, SEAM - 1, 1)):
        @pl.when(row == here)
        def _():
            all_tiles(beyond, b_send.at[0], b_recv).wait_recv()
            layer = raised_layers((3 * (1 - e),), spread_of(beyond[...]))
            raised_in[e] = packed(layer)
            for s in range(2):
                corner_out[s, 2 + e] = layer[96 * s : 96 * s + C1].astype(BF16)

    for e, here in ((0, SEAM), (1, SEAM - 1)):
        for s, dc in sides:
            copy = Shift(
                corner_out.at[s, 2 + e], corner_in.at[1 - s, e], s_send.at[s, e], s_recv.at[s, e], 0, dc
            )
            copy.there = jnp.logical_and(copy.there, row == here)
            copy.back = jnp.logical_and(copy.back, row == here)
            copy.start()
            joined_sends.append(copy)

    v_of = iota((256, WIDTH), 1)

    def shifted(value):
        v_ = v_of[: value.shape[0]]
        value = value.astype(F32)
        return (
            jnp.where(v_ == 0, 0.0, pltpu.roll(value, 1, 1)).astype(BF16),
            jnp.where(v_ == WIDTH - 1, 0.0, pltpu.roll(value, WIDTH - 1, 1)).astype(BF16),
        )

    def store_slab(i, layer, lift):
        joined = layer.astype(F32) + lift
        slabs[i, 1] = joined.astype(BF16)
        slabs[i, 0], slabs[i, 2] = shifted(joined.astype(BF16))

    for d in range(DEP):
        if d % 2 == 0:
            lift = dot(raise_h, raised[d // 2].astype(BF16))
        store_slab(1 + d, feat[d], lift)

    def windows(ref, d, first, last, size):
        return jnp.concatenate(
            [ref[d + i + first : d + i + last].reshape((last - first) * 3 * size, WIDTH) for i in range(2)], axis=1
        )

    spans = ((1, 3), (0, 3), (0, 3), (0, 2))
    for p, (first, last) in enumerate(spans):
        accs[p] = dot(band[:, first * 768 : last * 768], windows(slabs, 2 * p, first, last, 256))

    for copy in joined_sends:
        copy.wait()
    for e in range(2):
        store_slab(e * (DEP + 1), feat_in[e], dot(raise_h, unpacked(raised_in[e]).astype(BF16)))
    rims = [unpacked(rim_in[s]) for s in range(2)]
    for d in range(DEP + 2):
        rim = []
        for s in range(2):
            if d in (0, DEP + 1):
                lift = corner_in[s, d // (DEP + 1)].astype(F32)
            else:
                a = (d - 1) // 2
                lift = rims[s][a * C1 : (a + 1) * C1]
            rim.append((feat_rim_in[s, d].astype(F32) + lift).astype(BF16))
        rim = jnp.concatenate(rim, axis=0)
        edges[d, 1] = rim
        edges[d, 0], edges[d, 2] = shifted(rim)
    for p in range(4):
        total = accs[p] + dot(band_h[...], windows(edges, 2 * p, 0, 3, 64))
        if p == 0:
            total += dot(band[:, :768], windows(slabs, 0, 0, 1, 256))
        if p == 3:
            total += dot(band[:, 1536:], windows(slabs, 6, 2, 3, 256))
        total = silu(total).astype(BF16)
        out_ref[2 * p] = total[:, :WIDTH]
        out_ref[2 * p + 1] = total[:, WIDTH:]

    all_tiles(tiles.at[1], a_send, a_recv).wait_send()
    all_tiles(arrived, p_send, p_recv).wait_send()
    for i, to in enumerate((SEAM, SEAM - 1)):
        @pl.when(row != to)
        def _():
            beyond_copy(i, to).wait_send()


def body(features, down_weight, bott_weight, up_weight, dec_weight):
    dma = pltpu.SemaphoreType.DMA
    out = pl.pallas_call(
        kernel,
        out_shape=jax.ShapeDtypeStruct((DEP, 256, WIDTH), BF16),
        in_specs=[pl.BlockSpec(memory_space=pltpu.HBM)] * 5,
        out_specs=pl.BlockSpec(memory_space=pltpu.VMEM),
        scratch_shapes=[
            pltpu.VMEM((DEP, 256, WIDTH), BF16),
            pltpu.VMEM((16, 4, C1, CB), BF16),
            pltpu.VMEM((16, 4, C1, CB), BF16),
            pltpu.VMEM((27, C1, C1), BF16),
            pltpu.VMEM((27, 128, 128), BF16),
            pltpu.VMEM((4, WB, 128), BF16),
            pltpu.VMEM((3, ROWS + 2, WB, 128), BF16),
            pltpu.VMEM((ROWS, WB, 128), BF16),
            pltpu.VMEM((ROWS, WB, 128), BF16),
            pltpu.VMEM((256, 9 * 256), BF16),
            pltpu.VMEM((256, 9 * 64), BF16),
            pltpu.VMEM((DEP + 2, 3, 256, WIDTH), BF16),
            pltpu.VMEM((DEP + 2, 3, 64, WIDTH), BF16),
            pltpu.VMEM((DEP // 2, 256, 2 * WIDTH), F32),
            pltpu.VMEM((2, 256, WIDTH), BF16),
            pltpu.VMEM((2, DEP, C1, WIDTH), BF16),
            pltpu.VMEM((2, DEP + 2, C1, WIDTH), BF16),
            pltpu.VMEM((ROWS, WB, 128), BF16),
            pltpu.VMEM((2, 64, WIDTH), BF16),
            pltpu.VMEM((2, 64, WIDTH), BF16),
            pltpu.VMEM((2, 64, WIDTH), BF16),
            pltpu.VMEM((2, 64, WIDTH), BF16),
            pltpu.VMEM((2, 4, C1, WIDTH), BF16),
            pltpu.VMEM((2, 2, C1, WIDTH), BF16),
            dma((5,)), dma((6,)), dma((6,)), dma, dma, dma((2, 2)), dma((2, 2)), dma, dma, dma((2,)), dma,
            dma((8,)), dma((8,)), dma((8,)), dma((8,)), dma((2, 2)), dma((2, 2)),
        ],
        compiler_params=pltpu.CompilerParams(
            collective_id=0, has_side_effects=True, vmem_limit_bytes=60 * 1024 * 1024
        ),
        name="encode_decode",
    )(
        features.reshape(DEP, 256, WIDTH),
        down_weight.reshape(16, 4, C1, CB),
        bott_weight.reshape(27, CIN, CB),
        up_weight.reshape(16, 4, C1, CB),
        dec_weight.reshape(27, C1, C1),
    )
    return out.reshape(features.shape)


def solution(mesh):
    placed = (P("row", None, "col", None), P(), P(None, None, None, "row", None), P(), P())
    return jax.shard_map(
        body, mesh=mesh, in_specs=placed, out_specs=P("row", None, "col", None), check_vma=False
    )
```

```python
import jax
import jax.numpy as jnp
from jax import lax
from jax.experimental import pallas as pl
from jax.experimental.pallas import tpu as pltpu
from jax.sharding import PartitionSpec as P

MESH = pl.DeviceIdType.MESH
F32 = jnp.float32
BF16 = jnp.bfloat16
ROWS, COLS, GROUP = 32, 8, 4
C1, CB, WIDTH = 32, 512, 128
DEP, HGT, WB = 8, 8, 16
CIN = CB // ROWS
SEAM = ROWS // 2
NT = (((1,), (1,)), ((), ()))


def iota(shape, dim):
    return lax.broadcasted_iota(jnp.int32, shape, dim)


def ones_where(mask):
    return jnp.where(mask, 1.0, 0.0).astype(BF16)


def silu(v):
    return 0.5 * v * (1.0 + jnp.tanh(0.5 * v))


def dot(a, b):
    return jnp.dot(a, b, preferred_element_type=F32)


def dot_nt(a, b):
    return lax.dot_general(a, b, NT, preferred_element_type=F32)


def hops(offset):
    dz, dx, dy = offset
    return 4 * dz + min(dx, 4 - dx) + min(dy, 4 - dy)


PEERS = sorted(
    [(dz, dx, dy) for dz in range(2) for dx in range(4) for dy in range(4) if dz + dx + dy],
    key=hops,
    reverse=True,
)


def kernel(
    feat_hbm, down_hbm, bott_hbm, up_hbm, dec_hbm, out_ref,
    feat, down, up, dec, wg, lowered, tiles, part, arrived, band, band_h,
    slabs, edges, accs, feat_in, feat_rim, feat_rim_in, beyond,
    raised_out, raised_in, rim_out, rim_in, corner_out, corner_in,
    load_sem, w_send, w_recv, a_send, a_recv, h_send, h_recv, p_send, p_recv, b_send, b_recv,
    j_send, j_recv, f_send, f_recv, s_send, s_recv,
):
    row, col = lax.axis_index("row"), lax.axis_index("col")
    row_z, row_x, lane = row // 16, (row // GROUP) % 4, row % GROUP
    half = row_x % 2

    def device(r, c):
        return {"row": r, "col": c}

    def peer(offset):
        dz, dx, dy = offset
        return (row_z + dz) % 2 * 16 + (row_x + dx) % 4 * GROUP + (lane + dy) % GROUP

    barrier = pltpu.get_barrier_semaphore()

    def greet(r, c):
        pl.semaphore_signal(barrier, inc=1, device_id=device(r, c), device_id_type=MESH)

    for offset in PEERS:
        greet(peer(offset), col)
    for dr in (-1, 0, 1):
        for dc in (-1, 1):
            greet((row + dr + ROWS) % ROWS, (col + dc + COLS) % COLS)

    loads = [
        pltpu.make_async_copy(src, dst, load_sem.at[i])
        for i, (src, dst) in enumerate(
            [(feat_hbm, feat), (down_hbm, down), (dec_hbm, dec), (up_hbm, up)]
        )
    ]
    for load in loads:
        load.start()

    def weight_slot(owner_lane):
        start = pl.multiple_of(half * (GROUP * CIN) + owner_lane * CIN, CIN)
        return wg.at[:, pl.ds(start, CIN), :]

    def weight_piece(lane_to):
        return bott_hbm.at[:, :, pl.ds(pl.multiple_of(lane_to * 128, 128), 128)]

    own_weight = pltpu.make_async_copy(weight_piece(lane), weight_slot(lane), load_sem.at[4])
    own_weight.start()

    rest = pl.multiple_of((1 - half) * (GROUP * CIN), GROUP * CIN)
    wg[:, pl.ds(rest, GROUP * CIN), :] = jnp.zeros((27, GROUP * CIN, 128), BF16)
    tiles[:, 0] = jnp.zeros((3, WB, 128), BF16)
    tiles[:, ROWS + 1] = jnp.zeros((3, WB, 128), BF16)

    for side, edge in ((0, row == 0), (1, row == ROWS - 1)):
        @pl.when(edge)
        def _():
            feat_in[side] = jnp.zeros((256, WIDTH), BF16)
            raised_in[side] = jnp.zeros((64, WIDTH), BF16)
            feat_rim_in[:, side * (DEP + 1)] = jnp.zeros((2, C1, WIDTH), BF16)
            corner_in[:, side] = jnp.zeros((2, C1, WIDTH), BF16)

    for side, edge in ((0, col == 0), (1, col == COLS - 1)):
        @pl.when(edge)
        def _():
            tiles[2 * side] = jnp.zeros((ROWS + 2, WB, 128), BF16)
            feat_rim_in[side] = jnp.zeros((DEP + 2, C1, WIDTH), BF16)
            rim_in[side] = jnp.zeros((64, WIDTH), BF16)
            corner_in[side] = jnp.zeros((2, C1, WIDTH), BF16)

    def inside(dr, dc):
        yes = None
        for at, step, count in ((row, dr, ROWS), (col, dc, COLS)):
            if step:
                here = at > 0 if step < 0 else at < count - 1
                yes = here if yes is None else jnp.logical_and(yes, here)
        return yes

    def off_seam(dr):
        return row != SEAM - 1 if dr > 0 else row != SEAM

    class Shift:
        def __init__(self, src, dst, send, recv, dr, dc, seam=None):
            self.there, self.back = inside(dr, dc), inside(-dr, -dc)
            if seam is not None:
                self.there = jnp.logical_and(self.there, off_seam(dr))
                self.back = jnp.logical_and(self.back, off_seam(-dr))
            self.copy = pltpu.make_async_remote_copy(
                src_ref=src, dst_ref=dst, send_sem=send, recv_sem=recv,
                device_id=device((row + dr + ROWS) % ROWS, (col + dc + COLS) % COLS), device_id_type=MESH,
            )

        def start(self, also=None):
            @pl.when(self.there if also is None else jnp.logical_and(self.there, also))
            def _():
                self.copy.start()

        def wait(self):
            @pl.when(self.there)
            def _():
                self.copy.wait_send()

            @pl.when(self.back)
            def _():
                self.copy.wait_recv()

    loads[0].wait()
    r_, c_ = iota((128, 256), 0), iota((128, 256), 1)
    pool_h = ones_where(((r_ % C1) == (c_ // HGT)) & ((r_ // C1) == (c_ % HGT) // 2))
    pool_h = jnp.concatenate([pool_h, pool_h], axis=1)
    r_, c_ = iota((64, WIDTH), 0), iota((64, WIDTH), 1)
    pool_w = jnp.where((c_ // 2) == (r_ % WB) * 4 + r_ // WB, 0.125, 0.0).astype(BF16)
    pooled = []
    for a in range(4):
        pair = feat[2 * a : 2 * a + 2].reshape(512, WIDTH)
        pooled.append(dot_nt(pool_w, dot(pool_h, pair).astype(BF16)).astype(BF16))
    pooled = jnp.concatenate(pooled, axis=1)

    loads[1].wait()
    total = jnp.zeros((WB, CB), F32)
    for c in range(4):
        total += dot(pooled[c * WB : (c + 1) * WB], down[:, c].reshape(512, CB))
    low = silu(total).astype(BF16)
    for k in range(4):
        lowered[k] = low[:, k * 128 : (k + 1) * 128]

    r_, c_ = iota((64, 256), 0), iota((64, 256), 1)
    pick = ones_where(((c_ // HGT) == (r_ % C1)) & ((c_ % HGT) == (r_ // C1) * (HGT - 1)))
    for d in range(DEP):
        rim = dot(pick, feat[d]).astype(BF16)
        feat_rim[0, d] = rim[:C1]
        feat_rim[1, d] = rim[C1:]

    pl.semaphore_wait(barrier, ROWS - 1 + 6)

    for offset in PEERS:
        to = peer(offset)
        pltpu.make_async_remote_copy(
            src_ref=lowered.at[to // 8],
            dst_ref=tiles.at[1, 1 + row],
            send_sem=a_send,
            recv_sem=a_recv,
            device_id=device(to, col),
            device_id_type=MESH,
        ).start()

    weight_sends = []
    for j in range(1, GROUP):
        to = (lane + j) % GROUP
        copy = pltpu.make_async_remote_copy(
            src_ref=weight_piece(to),
            dst_ref=weight_slot(lane),
            send_sem=w_send.at[j - 1],
            recv_sem=w_recv.at[j - 1],
            device_id=device(row - lane + to, col),
            device_id_type=MESH,
        )
        copy.start()
        weight_sends.append(copy)

    sides, ends = ((0, -1), (1, 1)), ((0, -1, 0), (1, 1, DEP - 1))
    feat_moves = [(feat.at[d], feat_in.at[1 - e], dr, 0) for e, dr, d in ends]
    feat_moves += [(feat_rim.at[s], feat_rim_in.at[1 - s, pl.ds(1, DEP)], 0, dc) for s, dc in sides]
    feat_moves += [
        (feat_rim.at[s, d], feat_rim_in.at[1 - s, (1 - e) * (DEP + 1)], dr, dc) for s, dc in sides for e, dr, d in ends
    ]
    feat_sends = [
        Shift(src, dst, f_send.at[i], f_recv.at[i], dr, dc) for i, (src, dst, dr, dc) in enumerate(feat_moves)
    ]
    for copy in feat_sends:
        copy.start()

    tiles[1, 1 + row] = lowered[row // 8]

    loads[2].wait()
    r_, c_ = iota((256, C1), 0), iota((256, C1), 1)
    spread_o = ones_where((r_ // HGT) == c_)
    r_, c_ = iota((C1, 256), 0), iota((C1, 256), 1)
    spread_c = ones_where((c_ // HGT) == r_)
    shift = (iota((256, 256), 1) % HGT) - (iota((256, 256), 0) % HGT)
    h_of = iota((256, C1), 0) % HGT
    for kd in range(3):
        for kw in range(3):
            total = jnp.zeros((256, 256), F32)
            tops = []
            for kh in range(3):
                taps = dot_nt(spread_o, dec[(kd * 3 + kh) * 3 + kw]).astype(BF16)
                total = jnp.where(shift == kh - 1, dot(taps, spread_c), total)
                if kh != 1:
                    edge = 0 if kh == 0 else HGT - 1
                    tops.append(jnp.where(h_of == edge, taps.astype(F32), 0.0))
            at = kd * 3 + kw
            band[:, at * 256 : (at + 1) * 256] = total.astype(BF16)
            band_h[:, at * 64 : (at + 1) * 64] = jnp.concatenate(tops, axis=1).astype(BF16)

    def all_tiles(ref, send, recv):
        span = ref.at[pl.ds(1, ROWS - 1)]
        return pltpu.make_async_remote_copy(
            src_ref=span, dst_ref=span, send_sem=send, recv_sem=recv,
            device_id=device(peer(PEERS[0]), col), device_id_type=MESH,
        )

    all_tiles(tiles.at[1], a_send, a_recv).wait_recv()

    halo_sends = []
    for i, (start, size) in enumerate((((1 - row_z) * 15, 17), (row_z * 17, 15))):
        span = pl.ds(1 + start, size)
        halo_sends.append(
            [
                Shift(tiles.at[1, span], tiles.at[1 - dc, span], h_send.at[i, s], h_recv.at[i, s], 0, dc)
                for s, dc in enumerate((-1, 1))
            ]
        )
    for pair in halo_sends:
        for copy in pair:
            copy.start()

    own_weight.wait()
    for copy in weight_sends:
        copy.wait()

    def patches(heights, start):
        return jnp.concatenate(
            [tiles[b, pl.ds(start + a, 16)].reshape(256, 128) for a in range(3) for b in heights], axis=1
        )

    def taps_of(heights):
        return jnp.concatenate(
            [
                jnp.concatenate([wg[a * 9 + b * 3 + c] for a in range(3) for b in heights], axis=0)
                for c in range(3)
            ],
            axis=1,
        )

    def beyond_copy(i, to):
        return pltpu.make_async_remote_copy(
            src_ref=part.at[2 * SEAM - 1 - to], dst_ref=beyond.at[row],
            send_sem=b_send.at[i], recv_sem=b_recv, device_id=device(to, col), device_id_type=MESH,
        )

    starts = ((1 - row_z) * 16, row_z * 16)
    inner_taps = taps_of((1,))
    inner = [dot(patches((1,), start), inner_taps) for start in starts]
    w_of = iota((256, 128), 0) % WB
    for dz, start in ((1, starts[0]), (0, starts[1])):
        for copy in halo_sends[1 - dz]:
            copy.wait()
        partial = inner[1 - dz] + dot(patches((0, 2), start), taps_of((0, 2)))
        before = pltpu.roll(partial[:, :128], 1, 0)
        after = pltpu.roll(partial[:, 256:], 255, 0)
        summed = partial[:, 128:256] + jnp.where(w_of == 0, 0.0, before) + jnp.where(w_of == WB - 1, 0.0, after)
        part[pl.ds(start, 16)] = summed.astype(BF16).reshape(16, WB, 128)
        if dz == 0:
            for i, to in enumerate((SEAM, SEAM - 1)):
                @pl.when(row != to)
                def _():
                    beyond_copy(i, to).start()

                @pl.when(row == to)
                def _():
                    beyond[row] = part[2 * SEAM - 1 - to]

        for offset in PEERS:
            if offset[0] == dz:
                to = peer(offset)
                pltpu.make_async_remote_copy(
                    src_ref=part.at[to],
                    dst_ref=arrived.at[row],
                    send_sem=p_send,
                    recv_sem=p_recv,
                    device_id=device(to, col),
                    device_id_type=MESH,
                ).start()

    arrived[row] = part[row]
    r_, c_ = iota((WB, 512), 1), iota((WB, 512), 0)
    spread_w = ones_where((((r_ % WIDTH) // 8) == c_) & ((((r_ % WIDTH) // 2) % 4) == (r_ // WIDTH)))
    r_, c_ = iota((256, 128), 0), iota((256, 128), 1)
    raise_h = ones_where(((c_ % C1) == (r_ // HGT)) & ((c_ // C1) == (r_ % HGT) // 2))
    loads[3].wait()
    all_tiles(arrived, p_send, p_recv).wait_recv()

    def spread_of(shares):
        groups = shares.reshape(ROWS // GROUP, GROUP, WB, 128).astype(F32).sum(axis=0)
        middle = silu(jnp.concatenate([groups[k] for k in range(GROUP)], axis=1)).astype(BF16)
        across = lax.dot_general(middle, spread_w, (((0,), (0,)), ((), ())), preferred_element_type=F32)
        across = across.astype(BF16)
        return jnp.concatenate([across[:, c * WIDTH : (c + 1) * WIDTH] for c in range(4)], axis=0)

    def raised_layers(layers, spread):
        rows = [
            jnp.concatenate([up[a * 4 : a * 4 + 4, c].reshape(128, CB) for a in layers], axis=0) for c in range(4)
        ]
        return dot(jnp.concatenate(rows, axis=1), spread)

    odd = (iota((64, WIDTH), 1) % 2) == 1

    def packed(value):
        return jnp.where(odd, value[64:], value[:64]).astype(BF16)

    def unpacked(value):
        both = value.astype(F32)
        even_rows = jnp.where(odd, pltpu.roll(both, 1, 1), both)
        odd_rows = jnp.where(odd, both, pltpu.roll(both, WIDTH - 1, 1))
        return jnp.concatenate([even_rows, odd_rows], axis=0)

    spread = spread_of(arrived[...])
    raised = [None] * 4
    joined_sends = []

    def send(src, dst, dr, dc, seam=None):
        i = len(joined_sends)
        joined_sends.append(Shift(src, dst, j_send.at[i], j_recv.at[i], dr, dc, seam))
        joined_sends[-1].start()

    outer = raised_layers((0, 3), spread)
    raised[0], raised[3] = outer[:128], outer[128:]
    for e, dr, a in ((0, -1, 0), (1, 1, 3)):
        raised_out[e] = packed(raised[a])
        send(raised_out.at[e], raised_in.at[1 - e], dr, 0, False)
        for s, dc in sides:
            corner_out[s, e] = raised[a][96 * s : 96 * s + C1].astype(BF16)
            send(corner_out.at[s, e], corner_in.at[1 - s, 1 - e], dr, dc, False)
    inner = raised_layers((1, 2), spread)
    raised[1], raised[2] = inner[:128], inner[128:]
    for s, dc in sides:
        rim_out[s] = packed(jnp.concatenate([raised[a][96 * s : 96 * s + C1] for a in range(4)], axis=0))
        send(rim_out.at[s], rim_in.at[1 - s], 0, dc)

    for copy in feat_sends:
        copy.wait()

    for e, here, dr in ((0, SEAM, -1), (1, SEAM - 1, 1)):
        @pl.when(row == here)
        def _():
            all_tiles(beyond, b_send.at[0], b_recv).wait_recv()
            layer = raised_layers((3 * (1 - e),), spread_of(beyond[...]))
            raised_in[e] = packed(layer)
            for s in range(2):
                corner_out[s, 2 + e] = layer[96 * s : 96 * s + C1].astype(BF16)

    for e, here in ((0, SEAM), (1, SEAM - 1)):
        for s, dc in sides:
            copy = Shift(
                corner_out.at[s, 2 + e], corner_in.at[1 - s, e], s_send.at[s, e], s_recv.at[s, e], 0, dc
            )
            copy.there = jnp.logical_and(copy.there, row == here)
            copy.back = jnp.logical_and(copy.back, row == here)
            copy.start()
            joined_sends.append(copy)

    v_of = iota((256, WIDTH), 1)

    def shifted(value):
        v_ = v_of[: value.shape[0]]
        value = value.astype(F32)
        return (
            jnp.where(v_ == 0, 0.0, pltpu.roll(value, 1, 1)).astype(BF16),
            jnp.where(v_ == WIDTH - 1, 0.0, pltpu.roll(value, WIDTH - 1, 1)).astype(BF16),
        )

    def store_slab(i, layer, lift):
        joined = (layer.astype(F32) + lift).astype(BF16)
        slabs[i, 1] = joined
        slabs[i, 0], slabs[i, 2] = shifted(joined)

    for d in range(DEP):
        if d % 2 == 0:
            lift = dot(raise_h, raised[d // 2].astype(BF16))
        store_slab(1 + d, feat[d], lift)

    def windows(ref, d, first, last, size):
        return jnp.concatenate(
            [ref[d + i + first : d + i + last].reshape((last - first) * 3 * size, WIDTH) for i in range(2)], axis=1
        )

    spans = ((1, 3), (0, 3), (0, 3), (0, 2))
    for p, (first, last) in enumerate(spans):
        accs[p] = dot(band[:, first * 768 : last * 768], windows(slabs, 2 * p, first, last, 256))

    def store_rim(d, lifts):
        rim = [(feat_rim_in[s, d].astype(F32) + lifts[s]).astype(BF16) for s in range(2)]
        rim = jnp.concatenate(rim, axis=0)
        edges[d, 1] = rim
        edges[d, 0], edges[d, 2] = shifted(rim)

    def finish(p):
        total = accs[p] + dot(band_h[...], windows(edges, 2 * p, 0, 3, 64))
        if p == 0:
            total += dot(band[:, :768], windows(slabs, 0, 0, 1, 256))
        if p == 3:
            total += dot(band[:, 1536:], windows(slabs, 6, 2, 3, 256))
        total = silu(total).astype(BF16)
        out_ref[2 * p] = total[:, :WIDTH]
        out_ref[2 * p + 1] = total[:, WIDTH:]

    for copy in joined_sends[6:8]:
        copy.wait()
    rims = [unpacked(rim_in[s]) for s in range(2)]
    for d in range(DEP):
        a = d // 2
        store_rim(1 + d, [rims[s][a * C1 : (a + 1) * C1] for s in range(2)])
    for p in (1, 2):
        finish(p)

    for copy in joined_sends[:6] + joined_sends[8:]:
        copy.wait()
    for e in range(2):
        store_slab(e * (DEP + 1), feat_in[e], dot(raise_h, unpacked(raised_in[e]).astype(BF16)))
        store_rim(e * (DEP + 1), [corner_in[s, e].astype(F32) for s in range(2)])
    for p in (0, 3):
        finish(p)

    all_tiles(tiles.at[1], a_send, a_recv).wait_send()
    all_tiles(arrived, p_send, p_recv).wait_send()
    for i, to in enumerate((SEAM, SEAM - 1)):
        @pl.when(row != to)
        def _():
            beyond_copy(i, to).wait_send()


def body(features, down_weight, bott_weight, up_weight, dec_weight):
    dma = pltpu.SemaphoreType.DMA
    out = pl.pallas_call(
        kernel,
        out_shape=jax.ShapeDtypeStruct((DEP, 256, WIDTH), BF16),
        in_specs=[pl.BlockSpec(memory_space=pltpu.HBM)] * 5,
        out_specs=pl.BlockSpec(memory_space=pltpu.VMEM),
        scratch_shapes=[
            pltpu.VMEM((DEP, 256, WIDTH), BF16),
            pltpu.VMEM((16, 4, C1, CB), BF16),
            pltpu.VMEM((16, 4, C1, CB), BF16),
            pltpu.VMEM((27, C1, C1), BF16),
            pltpu.VMEM((27, 128, 128), BF16),
            pltpu.VMEM((4, WB, 128), BF16),
            pltpu.VMEM((3, ROWS + 2, WB, 128), BF16),
            pltpu.VMEM((ROWS, WB, 128), BF16),
            pltpu.VMEM((ROWS, WB, 128), BF16),
            pltpu.VMEM((256, 9 * 256), BF16),
            pltpu.VMEM((256, 9 * 64), BF16),
            pltpu.VMEM((DEP + 2, 3, 256, WIDTH), BF16),
            pltpu.VMEM((DEP + 2, 3, 64, WIDTH), BF16),
            pltpu.VMEM((DEP // 2, 256, 2 * WIDTH), F32),
            pltpu.VMEM((2, 256, WIDTH), BF16),
            pltpu.VMEM((2, DEP, C1, WIDTH), BF16),
            pltpu.VMEM((2, DEP + 2, C1, WIDTH), BF16),
            pltpu.VMEM((ROWS, WB, 128), BF16),
            pltpu.VMEM((2, 64, WIDTH), BF16),
            pltpu.VMEM((2, 64, WIDTH), BF16),
            pltpu.VMEM((2, 64, WIDTH), BF16),
            pltpu.VMEM((2, 64, WIDTH), BF16),
            pltpu.VMEM((2, 4, C1, WIDTH), BF16),
            pltpu.VMEM((2, 2, C1, WIDTH), BF16),
            dma((5,)), dma((6,)), dma((6,)), dma, dma, dma((2, 2)), dma((2, 2)), dma, dma, dma((2,)), dma,
            dma((8,)), dma((8,)), dma((8,)), dma((8,)), dma((2, 2)), dma((2, 2)),
        ],
        compiler_params=pltpu.CompilerParams(
            collective_id=0, has_side_effects=True, vmem_limit_bytes=60 * 1024 * 1024
        ),
        name="encode_decode",
    )(
        features.reshape(DEP, 256, WIDTH),
        down_weight.reshape(16, 4, C1, CB),
        bott_weight.reshape(27, CIN, CB),
        up_weight.reshape(16, 4, C1, CB),
        dec_weight.reshape(27, C1, C1),
    )
    return out.reshape(features.shape)


def solution(mesh):
    placed = (P("row", None, "col", None), P(), P(None, None, None, "row", None), P(), P())
    return jax.shard_map(
        body, mesh=mesh, in_specs=placed, out_specs=P("row", None, "col", None), check_vma=False
    )
```

```python
import jax
import jax.numpy as jnp
from jax import lax
from jax.experimental import pallas as pl
from jax.experimental.pallas import tpu as pltpu
from jax.sharding import PartitionSpec as P

MESH = pl.DeviceIdType.MESH
F32 = jnp.float32
BF16 = jnp.bfloat16
ROWS, COLS, GROUP = 32, 8, 4
C1, CB, WIDTH = 32, 512, 128
DEP, HGT, WB = 8, 8, 16
CIN = CB // ROWS
SEAM = ROWS // 2
NT = (((1,), (1,)), ((), ()))


def iota(shape, dim):
    return lax.broadcasted_iota(jnp.int32, shape, dim)


def ones_where(mask):
    return jnp.where(mask, 1.0, 0.0).astype(BF16)


def silu(v):
    return 0.5 * v * (1.0 + jnp.tanh(0.5 * v))


def dot(a, b):
    return jnp.dot(a, b, preferred_element_type=F32)


def dot_nt(a, b):
    return lax.dot_general(a, b, NT, preferred_element_type=F32)


def hops(offset):
    dz, dx, dy = offset
    return 4 * dz + min(dx, 4 - dx) + min(dy, 4 - dy)


PEERS = sorted(
    [(dz, dx, dy) for dz in range(2) for dx in range(4) for dy in range(4) if dz + dx + dy],
    key=hops,
    reverse=True,
)


def kernel(
    feat_hbm, down_hbm, bott_hbm, up_hbm, dec_hbm, out_ref,
    feat, down, up, dec, wg, lowered, tiles, part, arrived, band, band_h,
    slabs, edges, accs, feat_in, feat_rim, feat_rim_in, beyond,
    raised_out, raised_in, rim_out, rim_in, corner_out, corner_in,
    load_sem, w_send, w_recv, a_send, a_recv, h_send, h_recv, p_send, p_recv, b_send, b_recv,
    j_send, j_recv, f_send, f_recv, s_send, s_recv,
):
    row, col = lax.axis_index("row"), lax.axis_index("col")
    row_z, row_x, lane = row // 16, (row // GROUP) % 4, row % GROUP
    half = row_x % 2

    def device(r, c):
        return {"row": r, "col": c}

    def peer(offset):
        dz, dx, dy = offset
        return (row_z + dz) % 2 * 16 + (row_x + dx) % 4 * GROUP + (lane + dy) % GROUP

    barrier = pltpu.get_barrier_semaphore()

    def greet(r, c):
        pl.semaphore_signal(barrier, inc=1, device_id=device(r, c), device_id_type=MESH)

    for offset in PEERS:
        greet(peer(offset), col)
    for dr in (-1, 0, 1):
        for dc in (-1, 1):
            greet((row + dr + ROWS) % ROWS, (col + dc + COLS) % COLS)

    loads = [
        pltpu.make_async_copy(src, dst, load_sem.at[i])
        for i, (src, dst) in enumerate(
            [(feat_hbm, feat), (down_hbm, down), (dec_hbm, dec), (up_hbm, up)]
        )
    ]
    for load in loads:
        load.start()

    def weight_slot(owner_lane):
        start = pl.multiple_of(half * (GROUP * CIN) + owner_lane * CIN, CIN)
        return wg.at[:, pl.ds(start, CIN), :]

    def weight_piece(lane_to):
        return bott_hbm.at[:, :, pl.ds(pl.multiple_of(lane_to * 128, 128), 128)]

    own_weight = pltpu.make_async_copy(weight_piece(lane), weight_slot(lane), load_sem.at[4])
    own_weight.start()

    rest = pl.multiple_of((1 - half) * (GROUP * CIN), GROUP * CIN)
    wg[:, pl.ds(rest, GROUP * CIN), :] = jnp.zeros((27, GROUP * CIN, 128), BF16)
    tiles[:, 0] = jnp.zeros((3, WB, 128), BF16)
    tiles[:, ROWS + 1] = jnp.zeros((3, WB, 128), BF16)

    for side, edge in ((0, row == 0), (1, row == ROWS - 1)):
        @pl.when(edge)
        def _():
            feat_in[side] = jnp.zeros((256, WIDTH), BF16)
            raised_in[side] = jnp.zeros((64, WIDTH), BF16)
            feat_rim_in[:, side * (DEP + 1)] = jnp.zeros((2, C1, WIDTH), BF16)
            corner_in[:, side] = jnp.zeros((2, C1, WIDTH), BF16)

    for side, edge in ((0, col == 0), (1, col == COLS - 1)):
        @pl.when(edge)
        def _():
            tiles[2 * side] = jnp.zeros((ROWS + 2, WB, 128), BF16)
            feat_rim_in[side] = jnp.zeros((DEP + 2, C1, WIDTH), BF16)
            rim_in[side] = jnp.zeros((64, WIDTH), BF16)
            corner_in[side] = jnp.zeros((2, C1, WIDTH), BF16)

    def inside(dr, dc):
        yes = None
        for at, step, count in ((row, dr, ROWS), (col, dc, COLS)):
            if step:
                here = at > 0 if step < 0 else at < count - 1
                yes = here if yes is None else jnp.logical_and(yes, here)
        return yes

    def off_seam(dr):
        return row != SEAM - 1 if dr > 0 else row != SEAM

    class Shift:
        def __init__(self, src, dst, send, recv, dr, dc, seam=None):
            self.there, self.back = inside(dr, dc), inside(-dr, -dc)
            if seam is not None:
                self.there = jnp.logical_and(self.there, off_seam(dr))
                self.back = jnp.logical_and(self.back, off_seam(-dr))
            self.copy = pltpu.make_async_remote_copy(
                src_ref=src, dst_ref=dst, send_sem=send, recv_sem=recv,
                device_id=device((row + dr + ROWS) % ROWS, (col + dc + COLS) % COLS), device_id_type=MESH,
            )

        def start(self, also=None):
            @pl.when(self.there if also is None else jnp.logical_and(self.there, also))
            def _():
                self.copy.start()

        def wait(self):
            @pl.when(self.there)
            def _():
                self.copy.wait_send()

            @pl.when(self.back)
            def _():
                self.copy.wait_recv()

    loads[0].wait()
    r_, c_ = iota((128, 256), 0), iota((128, 256), 1)
    pool_h = ones_where(((r_ % C1) == (c_ // HGT)) & ((r_ // C1) == (c_ % HGT) // 2))
    pool_h = jnp.concatenate([pool_h, pool_h], axis=1)
    r_, c_ = iota((64, WIDTH), 0), iota((64, WIDTH), 1)
    pool_w = jnp.where((c_ // 2) == (r_ % WB) * 4 + r_ // WB, 0.125, 0.0).astype(BF16)
    pooled = []
    for a in range(4):
        pair = feat[2 * a : 2 * a + 2].reshape(512, WIDTH)
        pooled.append(dot_nt(pool_w, dot(pool_h, pair).astype(BF16)).astype(BF16))
    pooled = jnp.concatenate(pooled, axis=1)

    loads[1].wait()
    total = jnp.zeros((WB, CB), F32)
    for c in range(4):
        total += dot(pooled[c * WB : (c + 1) * WB], down[:, c].reshape(512, CB))
    low = silu(total).astype(BF16)
    for k in range(4):
        lowered[k] = low[:, k * 128 : (k + 1) * 128]

    r_, c_ = iota((64, 256), 0), iota((64, 256), 1)
    pick = ones_where(((c_ // HGT) == (r_ % C1)) & ((c_ % HGT) == (r_ // C1) * (HGT - 1)))
    for d in range(DEP):
        rim = dot(pick, feat[d]).astype(BF16)
        feat_rim[0, d] = rim[:C1]
        feat_rim[1, d] = rim[C1:]

    pl.semaphore_wait(barrier, ROWS - 1 + 6)

    for offset in PEERS:
        to = peer(offset)
        pltpu.make_async_remote_copy(
            src_ref=lowered.at[to // 8],
            dst_ref=tiles.at[1, 1 + row],
            send_sem=a_send,
            recv_sem=a_recv.at[offset[0]],
            device_id=device(to, col),
            device_id_type=MESH,
        ).start()

    weight_sends = []
    for j in range(1, GROUP):
        to = (lane + j) % GROUP
        copy = pltpu.make_async_remote_copy(
            src_ref=weight_piece(to),
            dst_ref=weight_slot(lane),
            send_sem=w_send.at[j - 1],
            recv_sem=w_recv.at[j - 1],
            device_id=device(row - lane + to, col),
            device_id_type=MESH,
        )
        copy.start()
        weight_sends.append(copy)

    sides, ends = ((0, -1), (1, 1)), ((0, -1, 0), (1, 1, DEP - 1))
    feat_moves = [(feat.at[d], feat_in.at[1 - e], dr, 0) for e, dr, d in ends]
    feat_moves += [(feat_rim.at[s], feat_rim_in.at[1 - s, pl.ds(1, DEP)], 0, dc) for s, dc in sides]
    feat_moves += [
        (feat_rim.at[s, d], feat_rim_in.at[1 - s, (1 - e) * (DEP + 1)], dr, dc) for s, dc in sides for e, dr, d in ends
    ]
    feat_sends = [
        Shift(src, dst, f_send.at[i], f_recv.at[i], dr, dc) for i, (src, dst, dr, dc) in enumerate(feat_moves)
    ]
    for copy in feat_sends:
        copy.start()

    tiles[1, 1 + row] = lowered[row // 8]

    loads[2].wait()
    r_, c_ = iota((256, C1), 0), iota((256, C1), 1)
    spread_o = ones_where((r_ // HGT) == c_)
    r_, c_ = iota((C1, 256), 0), iota((C1, 256), 1)
    spread_c = ones_where((c_ // HGT) == r_)
    shift = (iota((256, 256), 1) % HGT) - (iota((256, 256), 0) % HGT)
    h_of = iota((256, C1), 0) % HGT
    for kd in range(3):
        for kw in range(3):
            total = jnp.zeros((256, 256), F32)
            tops = []
            for kh in range(3):
                taps = dot_nt(spread_o, dec[(kd * 3 + kh) * 3 + kw]).astype(BF16)
                total = jnp.where(shift == kh - 1, dot(taps, spread_c), total)
                if kh != 1:
                    edge = 0 if kh == 0 else HGT - 1
                    tops.append(jnp.where(h_of == edge, taps.astype(F32), 0.0))
            at = kd * 3 + kw
            band[:, at * 256 : (at + 1) * 256] = total.astype(BF16)
            band_h[:, at * 64 : (at + 1) * 64] = jnp.concatenate(tops, axis=1).astype(BF16)

    def all_tiles(ref, send, recv):
        span = ref.at[pl.ds(1, ROWS - 1)]
        return pltpu.make_async_remote_copy(
            src_ref=span, dst_ref=span, send_sem=send, recv_sem=recv,
            device_id=device(peer(PEERS[0]), col), device_id_type=MESH,
        )

    halo_sends = []
    for dz in range(2):
        start = 1 + (row_z + dz) % 2 * SEAM
        span, come = pl.ds(start, SEAM), tiles.at[1, pl.ds(start, SEAM - 1 + dz)]
        pltpu.make_async_remote_copy(
            src_ref=come, dst_ref=come, send_sem=a_send, recv_sem=a_recv.at[dz],
            device_id=device(peer(PEERS[0]), col), device_id_type=MESH,
        ).wait_recv()
        halo_sends.append(
            [
                Shift(tiles.at[1, span], tiles.at[1 - dc, span], h_send.at[dz, s], h_recv.at[dz, s], 0, dc)
                for s, dc in enumerate((-1, 1))
            ]
        )
        for copy in halo_sends[dz]:
            copy.start()

    own_weight.wait()
    for copy in weight_sends:
        copy.wait()

    def patches(heights, start):
        return jnp.concatenate(
            [tiles[b, pl.ds(start + a, 16)].reshape(256, 128) for a in range(3) for b in heights], axis=1
        )

    def taps_of(heights):
        return jnp.concatenate(
            [
                jnp.concatenate([wg[a * 9 + b * 3 + c] for a in range(3) for b in heights], axis=0)
                for c in range(3)
            ],
            axis=1,
        )

    def beyond_copy(i, to):
        return pltpu.make_async_remote_copy(
            src_ref=part.at[2 * SEAM - 1 - to], dst_ref=beyond.at[row],
            send_sem=b_send.at[i], recv_sem=b_recv, device_id=device(to, col), device_id_type=MESH,
        )

    starts = ((1 - row_z) * 16, row_z * 16)
    inner_taps = taps_of((1,))
    inner = [dot(patches((1,), start), inner_taps) for start in starts]
    w_of = iota((256, 128), 0) % WB
    for copy in halo_sends[0] + halo_sends[1]:
        copy.wait()
    for dz, start in ((1, starts[0]), (0, starts[1])):
        partial = inner[1 - dz] + dot(patches((0, 2), start), taps_of((0, 2)))
        before = pltpu.roll(partial[:, :128], 1, 0)
        after = pltpu.roll(partial[:, 256:], 255, 0)
        summed = partial[:, 128:256] + jnp.where(w_of == 0, 0.0, before) + jnp.where(w_of == WB - 1, 0.0, after)
        part[pl.ds(start, 16)] = summed.astype(BF16).reshape(16, WB, 128)
        if dz == 0:
            for i, to in enumerate((SEAM, SEAM - 1)):
                @pl.when(row != to)
                def _():
                    beyond_copy(i, to).start()

                @pl.when(row == to)
                def _():
                    beyond[row] = part[2 * SEAM - 1 - to]

        for offset in PEERS:
            if offset[0] == dz:
                to = peer(offset)
                pltpu.make_async_remote_copy(
                    src_ref=part.at[to],
                    dst_ref=arrived.at[row],
                    send_sem=p_send,
                    recv_sem=p_recv,
                    device_id=device(to, col),
                    device_id_type=MESH,
                ).start()

    arrived[row] = part[row]
    r_, c_ = iota((WB, 512), 1), iota((WB, 512), 0)
    spread_w = ones_where((((r_ % WIDTH) // 8) == c_) & ((((r_ % WIDTH) // 2) % 4) == (r_ // WIDTH)))
    r_, c_ = iota((256, 128), 0), iota((256, 128), 1)
    raise_h = ones_where(((c_ % C1) == (r_ // HGT)) & ((c_ // C1) == (r_ % HGT) // 2))
    loads[3].wait()
    all_tiles(arrived, p_send, p_recv).wait_recv()

    def spread_of(shares):
        groups = shares.reshape(ROWS // GROUP, GROUP, WB, 128).astype(F32).sum(axis=0)
        middle = silu(jnp.concatenate([groups[k] for k in range(GROUP)], axis=1)).astype(BF16)
        across = lax.dot_general(middle, spread_w, (((0,), (0,)), ((), ())), preferred_element_type=F32)
        across = across.astype(BF16)
        return jnp.concatenate([across[:, c * WIDTH : (c + 1) * WIDTH] for c in range(4)], axis=0)

    def raised_layers(layers, spread):
        rows = [
            jnp.concatenate([up[a * 4 : a * 4 + 4, c].reshape(128, CB) for a in layers], axis=0) for c in range(4)
        ]
        return dot(jnp.concatenate(rows, axis=1), spread)

    odd = (iota((64, WIDTH), 1) % 2) == 1

    def packed(value):
        return jnp.where(odd, value[64:], value[:64]).astype(BF16)

    def unpacked(value):
        both = value.astype(F32)
        even_rows = jnp.where(odd, pltpu.roll(both, 1, 1), both)
        odd_rows = jnp.where(odd, both, pltpu.roll(both, WIDTH - 1, 1))
        return jnp.concatenate([even_rows, odd_rows], axis=0)

    spread = spread_of(arrived[...])
    raised = [None] * 4
    joined_sends = []

    def send(src, dst, dr, dc, seam=None):
        i = len(joined_sends)
        joined_sends.append(Shift(src, dst, j_send.at[i], j_recv.at[i], dr, dc, seam))
        joined_sends[-1].start()

    outer = raised_layers((0, 3), spread)
    raised[0], raised[3] = outer[:128], outer[128:]
    for e, dr, a in ((0, -1, 0), (1, 1, 3)):
        raised_out[e] = packed(raised[a])
        send(raised_out.at[e], raised_in.at[1 - e], dr, 0, False)
        for s, dc in sides:
            corner_out[s, e] = raised[a][96 * s : 96 * s + C1].astype(BF16)
            send(corner_out.at[s, e], corner_in.at[1 - s, 1 - e], dr, dc, False)
    inner = raised_layers((1, 2), spread)
    raised[1], raised[2] = inner[:128], inner[128:]
    for s, dc in sides:
        rim_out[s] = packed(jnp.concatenate([raised[a][96 * s : 96 * s + C1] for a in range(4)], axis=0))
        send(rim_out.at[s], rim_in.at[1 - s], 0, dc)

    for copy in feat_sends:
        copy.wait()

    for e, here, dr in ((0, SEAM, -1), (1, SEAM - 1, 1)):
        @pl.when(row == here)
        def _():
            all_tiles(beyond, b_send.at[0], b_recv).wait_recv()
            layer = raised_layers((3 * (1 - e),), spread_of(beyond[...]))
            raised_in[e] = packed(layer)
            for s in range(2):
                corner_out[s, 2 + e] = layer[96 * s : 96 * s + C1].astype(BF16)

    for e, here in ((0, SEAM), (1, SEAM - 1)):
        for s, dc in sides:
            copy = Shift(
                corner_out.at[s, 2 + e], corner_in.at[1 - s, e], s_send.at[s, e], s_recv.at[s, e], 0, dc
            )
            copy.there = jnp.logical_and(copy.there, row == here)
            copy.back = jnp.logical_and(copy.back, row == here)
            copy.start()
            joined_sends.append(copy)

    v_of = iota((256, WIDTH), 1)

    def shifted(value):
        v_ = v_of[: value.shape[0]]
        value = value.astype(F32)
        return (
            jnp.where(v_ == 0, 0.0, pltpu.roll(value, 1, 1)).astype(BF16),
            jnp.where(v_ == WIDTH - 1, 0.0, pltpu.roll(value, WIDTH - 1, 1)).astype(BF16),
        )

    def store_slab(i, layer, lift):
        joined = (layer.astype(F32) + lift).astype(BF16)
        slabs[i, 1] = joined
        slabs[i, 0], slabs[i, 2] = shifted(joined)

    for d in range(DEP):
        if d % 2 == 0:
            lift = dot(raise_h, raised[d // 2].astype(BF16))
        store_slab(1 + d, feat[d], lift)

    def windows(ref, d, first, last, size):
        return jnp.concatenate(
            [ref[d + i + first : d + i + last].reshape((last - first) * 3 * size, WIDTH) for i in range(2)], axis=1
        )

    spans = ((1, 3), (0, 3), (0, 3), (0, 2))
    for p, (first, last) in enumerate(spans):
        accs[p] = dot(band[:, first * 768 : last * 768], windows(slabs, 2 * p, first, last, 256))

    def store_rim(d, lifts):
        rim = [(feat_rim_in[s, d].astype(F32) + lifts[s]).astype(BF16) for s in range(2)]
        rim = jnp.concatenate(rim, axis=0)
        edges[d, 1] = rim
        edges[d, 0], edges[d, 2] = shifted(rim)

    def finish(p):
        total = accs[p] + dot(band_h[...], windows(edges, 2 * p, 0, 3, 64))
        if p == 0:
            total += dot(band[:, :768], windows(slabs, 0, 0, 1, 256))
        if p == 3:
            total += dot(band[:, 1536:], windows(slabs, 6, 2, 3, 256))
        total = silu(total).astype(BF16)
        out_ref[2 * p] = total[:, :WIDTH]
        out_ref[2 * p + 1] = total[:, WIDTH:]

    for copy in joined_sends[6:8]:
        copy.wait()
    rims = [unpacked(rim_in[s]) for s in range(2)]
    for d in range(DEP):
        a = d // 2
        store_rim(1 + d, [rims[s][a * C1 : (a + 1) * C1] for s in range(2)])
    for p in (1, 2):
        finish(p)

    for copy in joined_sends[:6] + joined_sends[8:]:
        copy.wait()
    for e in range(2):
        store_slab(e * (DEP + 1), feat_in[e], dot(raise_h, unpacked(raised_in[e]).astype(BF16)))
        store_rim(e * (DEP + 1), [corner_in[s, e].astype(F32) for s in range(2)])
    for p in (0, 3):
        finish(p)

    all_tiles(tiles.at[1], a_send, a_recv.at[0]).wait_send()
    all_tiles(arrived, p_send, p_recv).wait_send()
    for i, to in enumerate((SEAM, SEAM - 1)):
        @pl.when(row != to)
        def _():
            beyond_copy(i, to).wait_send()


def body(features, down_weight, bott_weight, up_weight, dec_weight):
    dma = pltpu.SemaphoreType.DMA
    out = pl.pallas_call(
        kernel,
        out_shape=jax.ShapeDtypeStruct((DEP, 256, WIDTH), BF16),
        in_specs=[pl.BlockSpec(memory_space=pltpu.HBM)] * 5,
        out_specs=pl.BlockSpec(memory_space=pltpu.VMEM),
        scratch_shapes=[
            pltpu.VMEM((DEP, 256, WIDTH), BF16),
            pltpu.VMEM((16, 4, C1, CB), BF16),
            pltpu.VMEM((16, 4, C1, CB), BF16),
            pltpu.VMEM((27, C1, C1), BF16),
            pltpu.VMEM((27, 128, 128), BF16),
            pltpu.VMEM((4, WB, 128), BF16),
            pltpu.VMEM((3, ROWS + 2, WB, 128), BF16),
            pltpu.VMEM((ROWS, WB, 128), BF16),
            pltpu.VMEM((ROWS, WB, 128), BF16),
            pltpu.VMEM((256, 9 * 256), BF16),
            pltpu.VMEM((256, 9 * 64), BF16),
            pltpu.VMEM((DEP + 2, 3, 256, WIDTH), BF16),
            pltpu.VMEM((DEP + 2, 3, 64, WIDTH), BF16),
            pltpu.VMEM((DEP // 2, 256, 2 * WIDTH), F32),
            pltpu.VMEM((2, 256, WIDTH), BF16),
            pltpu.VMEM((2, DEP, C1, WIDTH), BF16),
            pltpu.VMEM((2, DEP + 2, C1, WIDTH), BF16),
            pltpu.VMEM((ROWS, WB, 128), BF16),
            pltpu.VMEM((2, 64, WIDTH), BF16),
            pltpu.VMEM((2, 64, WIDTH), BF16),
            pltpu.VMEM((2, 64, WIDTH), BF16),
            pltpu.VMEM((2, 64, WIDTH), BF16),
            pltpu.VMEM((2, 4, C1, WIDTH), BF16),
            pltpu.VMEM((2, 2, C1, WIDTH), BF16),
            dma((5,)), dma((6,)), dma((6,)), dma, dma((2,)), dma((2, 2)), dma((2, 2)), dma, dma, dma((2,)), dma,
            dma((8,)), dma((8,)), dma((8,)), dma((8,)), dma((2, 2)), dma((2, 2)),
        ],
        compiler_params=pltpu.CompilerParams(
            collective_id=0, has_side_effects=True, vmem_limit_bytes=60 * 1024 * 1024
        ),
        name="encode_decode",
    )(
        features.reshape(DEP, 256, WIDTH),
        down_weight.reshape(16, 4, C1, CB),
        bott_weight.reshape(27, CIN, CB),
        up_weight.reshape(16, 4, C1, CB),
        dec_weight.reshape(27, C1, C1),
    )
    return out.reshape(features.shape)


def solution(mesh):
    placed = (P("row", None, "col", None), P(), P(None, None, None, "row", None), P(), P())
    return jax.shard_map(
        body, mesh=mesh, in_specs=placed, out_specs=P("row", None, "col", None), check_vma=False
    )
```

```python
import jax
import jax.numpy as jnp
from jax import lax
from jax.experimental import pallas as pl
from jax.experimental.pallas import tpu as pltpu
from jax.sharding import PartitionSpec as P

MESH = pl.DeviceIdType.MESH
F32 = jnp.float32
BF16 = jnp.bfloat16
ROWS, COLS, GROUP = 32, 8, 4
C1, CB, WIDTH = 32, 512, 128
DEP, HGT, WB = 8, 8, 16
CIN = CB // ROWS
SEAM = ROWS // 2
NT = (((1,), (1,)), ((), ()))


def iota(shape, dim):
    return lax.broadcasted_iota(jnp.int32, shape, dim)


def ones_where(mask):
    return jnp.where(mask, 1.0, 0.0).astype(BF16)


def silu(v):
    return 0.5 * v * (1.0 + jnp.tanh(0.5 * v))


def dot(a, b):
    return jnp.dot(a, b, preferred_element_type=F32)


def dot_nt(a, b):
    return lax.dot_general(a, b, NT, preferred_element_type=F32)


def hops(offset):
    dz, dx, dy = offset
    return 4 * dz + min(dx, 4 - dx) + min(dy, 4 - dy)


PEERS = sorted(
    [(dz, dx, dy) for dz in range(2) for dx in range(4) for dy in range(4) if dz + dx + dy],
    key=hops,
    reverse=True,
)


def kernel(
    feat_hbm, down_hbm, bott_hbm, up_hbm, dec_hbm, out_ref,
    feat, down, up, dec, wg, lowered, tiles, part, arrived, band, band_h,
    slabs, edges, accs, feat_in, feat_rim, feat_rim_in, beyond,
    raised_out, raised_in, rim_out, rim_in, corner_out, corner_in,
    load_sem, w_send, w_recv, a_send, a_recv, h_send, h_recv, p_send, p_recv, b_send, b_recv,
    j_send, j_recv, f_send, f_recv, s_send, s_recv,
):
    row, col = lax.axis_index("row"), lax.axis_index("col")
    row_z, row_x, lane = row // 16, (row // GROUP) % 4, row % GROUP
    half = row_x % 2

    def device(r, c):
        return {"row": r, "col": c}

    def peer(offset):
        dz, dx, dy = offset
        return (row_z + dz) % 2 * 16 + (row_x + dx) % 4 * GROUP + (lane + dy) % GROUP

    barrier = pltpu.get_barrier_semaphore()

    def greet(r, c):
        pl.semaphore_signal(barrier, inc=1, device_id=device(r, c), device_id_type=MESH)

    for offset in PEERS:
        greet(peer(offset), col)
    for dr in (-1, 0, 1):
        for dc in (-1, 1):
            greet((row + dr + ROWS) % ROWS, (col + dc + COLS) % COLS)

    loads = [
        pltpu.make_async_copy(src, dst, load_sem.at[i])
        for i, (src, dst) in enumerate(
            [(feat_hbm, feat), (down_hbm, down), (dec_hbm, dec), (up_hbm, up)]
        )
    ]
    for load in loads:
        load.start()

    def weight_slot(owner_lane):
        start = pl.multiple_of(half * (GROUP * CIN) + owner_lane * CIN, CIN)
        return wg.at[:, pl.ds(start, CIN), :]

    def weight_piece(lane_to):
        return bott_hbm.at[:, :, pl.ds(pl.multiple_of(lane_to * 128, 128), 128)]

    own_weight = pltpu.make_async_copy(weight_piece(lane), weight_slot(lane), load_sem.at[4])
    own_weight.start()

    rest = pl.multiple_of((1 - half) * (GROUP * CIN), GROUP * CIN)
    wg[:, pl.ds(rest, GROUP * CIN), :] = jnp.zeros((27, GROUP * CIN, 128), BF16)
    tiles[:, 0] = jnp.zeros((3, WB, 128), BF16)
    tiles[:, ROWS + 1] = jnp.zeros((3, WB, 128), BF16)

    for side, edge in ((0, row == 0), (1, row == ROWS - 1)):
        @pl.when(edge)
        def _():
            feat_in[side] = jnp.zeros((256, WIDTH), BF16)
            raised_in[side] = jnp.zeros((64, WIDTH), BF16)
            feat_rim_in[:, side * (DEP + 1)] = jnp.zeros((2, C1, WIDTH), BF16)
            corner_in[:, side] = jnp.zeros((2, C1, WIDTH), BF16)

    for side, edge in ((0, col == 0), (1, col == COLS - 1)):
        @pl.when(edge)
        def _():
            tiles[2 * side] = jnp.zeros((ROWS + 2, WB, 128), BF16)
            feat_rim_in[side] = jnp.zeros((DEP + 2, C1, WIDTH), BF16)
            rim_in[side] = jnp.zeros((64, WIDTH), BF16)
            corner_in[side] = jnp.zeros((2, C1, WIDTH), BF16)

    def inside(dr, dc):
        yes = None
        for at, step, count in ((row, dr, ROWS), (col, dc, COLS)):
            if step:
                here = at > 0 if step < 0 else at < count - 1
                yes = here if yes is None else jnp.logical_and(yes, here)
        return yes

    def off_seam(dr):
        return row != SEAM - 1 if dr > 0 else row != SEAM

    class Shift:
        def __init__(self, src, dst, send, recv, dr, dc, seam=None):
            self.there, self.back = inside(dr, dc), inside(-dr, -dc)
            if seam is not None:
                self.there = jnp.logical_and(self.there, off_seam(dr))
                self.back = jnp.logical_and(self.back, off_seam(-dr))
            self.copy = pltpu.make_async_remote_copy(
                src_ref=src, dst_ref=dst, send_sem=send, recv_sem=recv,
                device_id=device((row + dr + ROWS) % ROWS, (col + dc + COLS) % COLS), device_id_type=MESH,
            )

        def start(self, also=None):
            @pl.when(self.there if also is None else jnp.logical_and(self.there, also))
            def _():
                self.copy.start()

        def wait(self):
            @pl.when(self.there)
            def _():
                self.copy.wait_send()

            @pl.when(self.back)
            def _():
                self.copy.wait_recv()

    loads[0].wait()
    r_, c_ = iota((128, 256), 0), iota((128, 256), 1)
    pool_h = ones_where(((r_ % C1) == (c_ // HGT)) & ((r_ // C1) == (c_ % HGT) // 2))
    pool_h = jnp.concatenate([pool_h, pool_h], axis=1)
    r_, c_ = iota((64, WIDTH), 0), iota((64, WIDTH), 1)
    pool_w = jnp.where((c_ // 2) == (r_ % WB) * 4 + r_ // WB, 0.125, 0.0).astype(BF16)
    pooled = []
    for a in range(4):
        pair = feat[2 * a : 2 * a + 2].reshape(512, WIDTH)
        pooled.append(dot_nt(pool_w, dot(pool_h, pair).astype(BF16)).astype(BF16))
    pooled = jnp.concatenate(pooled, axis=1)

    loads[1].wait()
    total = jnp.zeros((WB, CB), F32)
    for c in range(4):
        total += dot(pooled[c * WB : (c + 1) * WB], down[:, c].reshape(512, CB))
    low = silu(total).astype(BF16)
    for k in range(4):
        lowered[k] = low[:, k * 128 : (k + 1) * 128]

    r_, c_ = iota((64, 256), 0), iota((64, 256), 1)
    pick = ones_where(((c_ // HGT) == (r_ % C1)) & ((c_ % HGT) == (r_ // C1) * (HGT - 1)))
    for d in range(DEP):
        rim = dot(pick, feat[d]).astype(BF16)
        feat_rim[0, d] = rim[:C1]
        feat_rim[1, d] = rim[C1:]

    pl.semaphore_wait(barrier, ROWS - 1 + 6)

    for offset in PEERS:
        to = peer(offset)
        pltpu.make_async_remote_copy(
            src_ref=lowered.at[to // 8],
            dst_ref=tiles.at[1, 1 + row],
            send_sem=a_send,
            recv_sem=a_recv,
            device_id=device(to, col),
            device_id_type=MESH,
        ).start()

    core = col % 2

    def taps_at(ref, start, size):
        return ref.at[pl.ds(start, size)]

    weight_sends = []
    for j in range(1, GROUP):
        to = (lane + j) % GROUP
        copy = pltpu.make_async_remote_copy(
            src_ref=taps_at(weight_piece(to), core * 13, 14),
            dst_ref=taps_at(weight_slot(lane), core * 13, 14),
            send_sem=w_send.at[j - 1],
            recv_sem=w_recv.at[j - 1],
            device_id=device(row - lane + to, col),
            device_id_type=MESH,
        )
        copy.start()
        weight_sends.append(copy)
    twin_sends = []
    for j in range(1, GROUP):
        slot = taps_at(weight_slot((lane + j) % GROUP), core * 14, 13)
        twin_sends.append(
            pltpu.make_async_remote_copy(
                src_ref=slot, dst_ref=slot, send_sem=w_send.at[GROUP + j - 2], recv_sem=w_recv.at[GROUP + j - 2],
                device_id=device(row, col + 1 - 2 * core), device_id_type=MESH,
            )
        )

    sides, ends = ((0, -1), (1, 1)), ((0, -1, 0), (1, 1, DEP - 1))
    feat_moves = [(feat.at[d], feat_in.at[1 - e], dr, 0) for e, dr, d in ends]
    feat_moves += [(feat_rim.at[s], feat_rim_in.at[1 - s, pl.ds(1, DEP)], 0, dc) for s, dc in sides]
    feat_moves += [
        (feat_rim.at[s, d], feat_rim_in.at[1 - s, (1 - e) * (DEP + 1)], dr, dc) for s, dc in sides for e, dr, d in ends
    ]
    feat_sends = [
        Shift(src, dst, f_send.at[i], f_recv.at[i], dr, dc) for i, (src, dst, dr, dc) in enumerate(feat_moves)
    ]
    for copy in feat_sends:
        copy.start()

    tiles[1, 1 + row] = lowered[row // 8]

    loads[2].wait()
    r_, c_ = iota((256, C1), 0), iota((256, C1), 1)
    spread_o = ones_where((r_ // HGT) == c_)
    r_, c_ = iota((C1, 256), 0), iota((C1, 256), 1)
    spread_c = ones_where((c_ // HGT) == r_)
    shift = (iota((256, 256), 1) % HGT) - (iota((256, 256), 0) % HGT)
    h_of = iota((256, C1), 0) % HGT
    for kd in range(3):
        for kw in range(3):
            total = jnp.zeros((256, 256), F32)
            tops = []
            for kh in range(3):
                taps = dot_nt(spread_o, dec[(kd * 3 + kh) * 3 + kw]).astype(BF16)
                total = jnp.where(shift == kh - 1, dot(taps, spread_c), total)
                if kh != 1:
                    edge = 0 if kh == 0 else HGT - 1
                    tops.append(jnp.where(h_of == edge, taps.astype(F32), 0.0))
            at = kd * 3 + kw
            band[:, at * 256 : (at + 1) * 256] = total.astype(BF16)
            band_h[:, at * 64 : (at + 1) * 64] = jnp.concatenate(tops, axis=1).astype(BF16)

    def all_tiles(ref, send, recv):
        span = ref.at[pl.ds(1, ROWS - 1)]
        return pltpu.make_async_remote_copy(
            src_ref=span, dst_ref=span, send_sem=send, recv_sem=recv,
            device_id=device(peer(PEERS[0]), col), device_id_type=MESH,
        )

    all_tiles(tiles.at[1], a_send, a_recv).wait_recv()

    halo_sends = []
    for i, (start, size) in enumerate((((1 - row_z) * 15, 17), (row_z * 17, 15))):
        span = pl.ds(1 + start, size)
        halo_sends.append(
            [
                Shift(tiles.at[1, span], tiles.at[1 - dc, span], h_send.at[i, s], h_recv.at[i, s], 0, dc)
                for s, dc in enumerate((-1, 1))
            ]
        )
    for pair in halo_sends:
        for copy in pair:
            copy.start()

    own_weight.wait()
    for copy in weight_sends:
        copy.wait()
    for copy in twin_sends:
        copy.start()
    for copy in twin_sends:
        copy.wait()

    def patches(heights, start):
        return jnp.concatenate(
            [tiles[b, pl.ds(start + a, 16)].reshape(256, 128) for a in range(3) for b in heights], axis=1
        )

    def taps_of(heights):
        return jnp.concatenate(
            [
                jnp.concatenate([wg[a * 9 + b * 3 + c] for a in range(3) for b in heights], axis=0)
                for c in range(3)
            ],
            axis=1,
        )

    def beyond_copy(i, to):
        return pltpu.make_async_remote_copy(
            src_ref=part.at[2 * SEAM - 1 - to], dst_ref=beyond.at[row],
            send_sem=b_send.at[i], recv_sem=b_recv, device_id=device(to, col), device_id_type=MESH,
        )

    starts = ((1 - row_z) * 16, row_z * 16)
    inner_taps = taps_of((1,))
    inner = [dot(patches((1,), start), inner_taps) for start in starts]
    w_of = iota((256, 128), 0) % WB
    for dz, start in ((1, starts[0]), (0, starts[1])):
        for copy in halo_sends[1 - dz]:
            copy.wait()
        partial = inner[1 - dz] + dot(patches((0, 2), start), taps_of((0, 2)))
        before = pltpu.roll(partial[:, :128], 1, 0)
        after = pltpu.roll(partial[:, 256:], 255, 0)
        summed = partial[:, 128:256] + jnp.where(w_of == 0, 0.0, before) + jnp.where(w_of == WB - 1, 0.0, after)
        part[pl.ds(start, 16)] = summed.astype(BF16).reshape(16, WB, 128)
        if dz == 0:
            for i, to in enumerate((SEAM, SEAM - 1)):
                @pl.when(row != to)
                def _():
                    beyond_copy(i, to).start()

                @pl.when(row == to)
                def _():
                    beyond[row] = part[2 * SEAM - 1 - to]

        for offset in PEERS:
            if offset[0] == dz:
                to = peer(offset)
                pltpu.make_async_remote_copy(
                    src_ref=part.at[to],
                    dst_ref=arrived.at[row],
                    send_sem=p_send,
                    recv_sem=p_recv,
                    device_id=device(to, col),
                    device_id_type=MESH,
                ).start()

    arrived[row] = part[row]
    r_, c_ = iota((WB, 512), 1), iota((WB, 512), 0)
    spread_w = ones_where((((r_ % WIDTH) // 8) == c_) & ((((r_ % WIDTH) // 2) % 4) == (r_ // WIDTH)))
    r_, c_ = iota((256, 128), 0), iota((256, 128), 1)
    raise_h = ones_where(((c_ % C1) == (r_ // HGT)) & ((c_ // C1) == (r_ % HGT) // 2))
    loads[3].wait()
    all_tiles(arrived, p_send, p_recv).wait_recv()

    def spread_of(shares):
        groups = shares.reshape(ROWS // GROUP, GROUP, WB, 128).astype(F32).sum(axis=0)
        middle = silu(jnp.concatenate([groups[k] for k in range(GROUP)], axis=1)).astype(BF16)
        across = lax.dot_general(middle, spread_w, (((0,), (0,)), ((), ())), preferred_element_type=F32)
        across = across.astype(BF16)
        return jnp.concatenate([across[:, c * WIDTH : (c + 1) * WIDTH] for c in range(4)], axis=0)

    def raised_layers(layers, spread):
        rows = [
            jnp.concatenate([up[a * 4 : a * 4 + 4, c].reshape(128, CB) for a in layers], axis=0) for c in range(4)
        ]
        return dot(jnp.concatenate(rows, axis=1), spread)

    odd = (iota((64, WIDTH), 1) % 2) == 1

    def packed(value):
        return jnp.where(odd, value[64:], value[:64]).astype(BF16)

    def unpacked(value):
        both = value.astype(F32)
        even_rows = jnp.where(odd, pltpu.roll(both, 1, 1), both)
        odd_rows = jnp.where(odd, both, pltpu.roll(both, WIDTH - 1, 1))
        return jnp.concatenate([even_rows, odd_rows], axis=0)

    spread = spread_of(arrived[...])
    raised = [None] * 4
    joined_sends = []

    def send(src, dst, dr, dc, seam=None):
        i = len(joined_sends)
        joined_sends.append(Shift(src, dst, j_send.at[i], j_recv.at[i], dr, dc, seam))
        joined_sends[-1].start()

    outer = raised_layers((0, 3), spread)
    raised[0], raised[3] = outer[:128], outer[128:]
    for e, dr, a in ((0, -1, 0), (1, 1, 3)):
        raised_out[e] = packed(raised[a])
        send(raised_out.at[e], raised_in.at[1 - e], dr, 0, False)
        for s, dc in sides:
            corner_out[s, e] = raised[a][96 * s : 96 * s + C1].astype(BF16)
            send(corner_out.at[s, e], corner_in.at[1 - s, 1 - e], dr, dc, False)
    inner = raised_layers((1, 2), spread)
    raised[1], raised[2] = inner[:128], inner[128:]
    for s, dc in sides:
        rim_out[s] = packed(jnp.concatenate([raised[a][96 * s : 96 * s + C1] for a in range(4)], axis=0))
        send(rim_out.at[s], rim_in.at[1 - s], 0, dc)

    for copy in feat_sends:
        copy.wait()

    for e, here, dr in ((0, SEAM, -1), (1, SEAM - 1, 1)):
        @pl.when(row == here)
        def _():
            all_tiles(beyond, b_send.at[0], b_recv).wait_recv()
            layer = raised_layers((3 * (1 - e),), spread_of(beyond[...]))
            raised_in[e] = packed(layer)
            for s in range(2):
                corner_out[s, 2 + e] = layer[96 * s : 96 * s + C1].astype(BF16)

    for e, here in ((0, SEAM), (1, SEAM - 1)):
        for s, dc in sides:
            copy = Shift(
                corner_out.at[s, 2 + e], corner_in.at[1 - s, e], s_send.at[s, e], s_recv.at[s, e], 0, dc
            )
            copy.there = jnp.logical_and(copy.there, row == here)
            copy.back = jnp.logical_and(copy.back, row == here)
            copy.start()
            joined_sends.append(copy)

    v_of = iota((256, WIDTH), 1)

    def shifted(value):
        v_ = v_of[: value.shape[0]]
        value = value.astype(F32)
        return (
            jnp.where(v_ == 0, 0.0, pltpu.roll(value, 1, 1)).astype(BF16),
            jnp.where(v_ == WIDTH - 1, 0.0, pltpu.roll(value, WIDTH - 1, 1)).astype(BF16),
        )

    def store_slab(i, layer, lift):
        joined = (layer.astype(F32) + lift).astype(BF16)
        slabs[i, 1] = joined
        slabs[i, 0], slabs[i, 2] = shifted(joined)

    for d in range(DEP):
        if d % 2 == 0:
            lift = dot(raise_h, raised[d // 2].astype(BF16))
        store_slab(1 + d, feat[d], lift)

    def windows(ref, d, first, last, size):
        return jnp.concatenate(
            [ref[d + i + first : d + i + last].reshape((last - first) * 3 * size, WIDTH) for i in range(2)], axis=1
        )

    spans = ((1, 3), (0, 3), (0, 3), (0, 2))
    for p, (first, last) in enumerate(spans):
        accs[p] = dot(band[:, first * 768 : last * 768], windows(slabs, 2 * p, first, last, 256))

    def store_rim(d, lifts):
        rim = [(feat_rim_in[s, d].astype(F32) + lifts[s]).astype(BF16) for s in range(2)]
        rim = jnp.concatenate(rim, axis=0)
        edges[d, 1] = rim
        edges[d, 0], edges[d, 2] = shifted(rim)

    def finish(p):
        total = accs[p] + dot(band_h[...], windows(edges, 2 * p, 0, 3, 64))
        if p == 0:
            total += dot(band[:, :768], windows(slabs, 0, 0, 1, 256))
        if p == 3:
            total += dot(band[:, 1536:], windows(slabs, 6, 2, 3, 256))
        total = silu(total).astype(BF16)
        out_ref[2 * p] = total[:, :WIDTH]
        out_ref[2 * p + 1] = total[:, WIDTH:]

    for copy in joined_sends[6:8]:
        copy.wait()
    rims = [unpacked(rim_in[s]) for s in range(2)]
    for d in range(DEP):
        a = d // 2
        store_rim(1 + d, [rims[s][a * C1 : (a + 1) * C1] for s in range(2)])
    for p in (1, 2):
        finish(p)

    for copy in joined_sends[:6] + joined_sends[8:]:
        copy.wait()
    for e in range(2):
        store_slab(e * (DEP + 1), feat_in[e], dot(raise_h, unpacked(raised_in[e]).astype(BF16)))
        store_rim(e * (DEP + 1), [corner_in[s, e].astype(F32) for s in range(2)])
    for p in (0, 3):
        finish(p)

    all_tiles(tiles.at[1], a_send, a_recv).wait_send()
    all_tiles(arrived, p_send, p_recv).wait_send()
    for i, to in enumerate((SEAM, SEAM - 1)):
        @pl.when(row != to)
        def _():
            beyond_copy(i, to).wait_send()


def body(features, down_weight, bott_weight, up_weight, dec_weight):
    dma = pltpu.SemaphoreType.DMA
    out = pl.pallas_call(
        kernel,
        out_shape=jax.ShapeDtypeStruct((DEP, 256, WIDTH), BF16),
        in_specs=[pl.BlockSpec(memory_space=pltpu.HBM)] * 5,
        out_specs=pl.BlockSpec(memory_space=pltpu.VMEM),
        scratch_shapes=[
            pltpu.VMEM((DEP, 256, WIDTH), BF16),
            pltpu.VMEM((16, 4, C1, CB), BF16),
            pltpu.VMEM((16, 4, C1, CB), BF16),
            pltpu.VMEM((27, C1, C1), BF16),
            pltpu.VMEM((27, 128, 128), BF16),
            pltpu.VMEM((4, WB, 128), BF16),
            pltpu.VMEM((3, ROWS + 2, WB, 128), BF16),
            pltpu.VMEM((ROWS, WB, 128), BF16),
            pltpu.VMEM((ROWS, WB, 128), BF16),
            pltpu.VMEM((256, 9 * 256), BF16),
            pltpu.VMEM((256, 9 * 64), BF16),
            pltpu.VMEM((DEP + 2, 3, 256, WIDTH), BF16),
            pltpu.VMEM((DEP + 2, 3, 64, WIDTH), BF16),
            pltpu.VMEM((DEP // 2, 256, 2 * WIDTH), F32),
            pltpu.VMEM((2, 256, WIDTH), BF16),
            pltpu.VMEM((2, DEP, C1, WIDTH), BF16),
            pltpu.VMEM((2, DEP + 2, C1, WIDTH), BF16),
            pltpu.VMEM((ROWS, WB, 128), BF16),
            pltpu.VMEM((2, 64, WIDTH), BF16),
            pltpu.VMEM((2, 64, WIDTH), BF16),
            pltpu.VMEM((2, 64, WIDTH), BF16),
            pltpu.VMEM((2, 64, WIDTH), BF16),
            pltpu.VMEM((2, 4, C1, WIDTH), BF16),
            pltpu.VMEM((2, 2, C1, WIDTH), BF16),
            dma((5,)), dma((6,)), dma((6,)), dma, dma, dma((2, 2)), dma((2, 2)), dma, dma, dma((2,)), dma,
            dma((8,)), dma((8,)), dma((8,)), dma((8,)), dma((2, 2)), dma((2, 2)),
        ],
        compiler_params=pltpu.CompilerParams(
            collective_id=0, has_side_effects=True, vmem_limit_bytes=60 * 1024 * 1024
        ),
        name="encode_decode",
    )(
        features.reshape(DEP, 256, WIDTH),
        down_weight.reshape(16, 4, C1, CB),
        bott_weight.reshape(27, CIN, CB),
        up_weight.reshape(16, 4, C1, CB),
        dec_weight.reshape(27, C1, C1),
    )
    return out.reshape(features.shape)


def solution(mesh):
    placed = (P("row", None, "col", None), P(), P(None, None, None, "row", None), P(), P())
    return jax.shard_map(
        body, mesh=mesh, in_specs=placed, out_specs=P("row", None, "col", None), check_vma=False
    )
```

```python
import jax
import jax.numpy as jnp
from jax import lax
from jax.experimental import pallas as pl
from jax.experimental.pallas import tpu as pltpu
from jax.sharding import PartitionSpec as P

MESH = pl.DeviceIdType.MESH
F32 = jnp.float32
BF16 = jnp.bfloat16
ROWS, COLS, GROUP = 32, 8, 4
C1, CB, WIDTH = 32, 512, 128
DEP, HGT, WB = 8, 8, 16
CIN = CB // ROWS
SEAM = ROWS // 2
NT = (((1,), (1,)), ((), ()))


def iota(shape, dim):
    return lax.broadcasted_iota(jnp.int32, shape, dim)


def ones_where(mask):
    return jnp.where(mask, 1.0, 0.0).astype(BF16)


def silu(v):
    return 0.5 * v * (1.0 + jnp.tanh(0.5 * v))


def dot(a, b):
    return jnp.dot(a, b, preferred_element_type=F32)


def dot_nt(a, b):
    return lax.dot_general(a, b, NT, preferred_element_type=F32)


def hops(offset):
    dz, dx, dy = offset
    return 4 * dz + min(dx, 4 - dx) + min(dy, 4 - dy)


PEERS = sorted(
    [(dz, dx, dy) for dz in range(2) for dx in range(4) for dy in range(4) if dz + dx + dy],
    key=hops,
    reverse=True,
)


def kernel(
    feat_hbm, down_hbm, bott_hbm, up_hbm, dec_hbm, out_ref,
    feat, down, up, dec, wg, lowered, tiles, part, arrived, band, band_h,
    slabs, edges, accs, feat_in, feat_rim, feat_rim_in, beyond,
    raised_out, raised_in, rim_out, rim_in, corner_out, corner_in,
    load_sem, w_send, w_recv, a_send, a_recv, h_send, h_recv, p_send, p_recv, b_send, b_recv,
    j_send, j_recv, f_send, f_recv, s_send, s_recv,
):
    row, col = lax.axis_index("row"), lax.axis_index("col")
    row_z, row_x, lane = row // 16, (row // GROUP) % 4, row % GROUP
    half = row_x % 2

    def device(r, c):
        return {"row": r, "col": c}

    def peer(offset):
        dz, dx, dy = offset
        return (row_z + dz) % 2 * 16 + (row_x + dx) % 4 * GROUP + (lane + dy) % GROUP

    barrier = pltpu.get_barrier_semaphore()

    def greet(r, c):
        pl.semaphore_signal(barrier, inc=1, device_id=device(r, c), device_id_type=MESH)

    for offset in PEERS:
        greet(peer(offset), col)
    for dr in (-1, 0, 1):
        for dc in (-1, 1):
            greet((row + dr + ROWS) % ROWS, (col + dc + COLS) % COLS)

    loads = [
        pltpu.make_async_copy(src, dst, load_sem.at[i])
        for i, (src, dst) in enumerate(
            [(feat_hbm, feat), (down_hbm, down), (dec_hbm, dec), (up_hbm, up)]
        )
    ]
    for load in loads:
        load.start()

    def weight_slot(owner_lane):
        start = pl.multiple_of(half * (GROUP * CIN) + owner_lane * CIN, CIN)
        return wg.at[:, pl.ds(start, CIN), :]

    def weight_piece(lane_to):
        return bott_hbm.at[:, :, pl.ds(pl.multiple_of(lane_to * 128, 128), 128)]

    own_weight = pltpu.make_async_copy(weight_piece(lane), weight_slot(lane), load_sem.at[4])
    own_weight.start()

    rest = pl.multiple_of((1 - half) * (GROUP * CIN), GROUP * CIN)
    wg[:, pl.ds(rest, GROUP * CIN), :] = jnp.zeros((27, GROUP * CIN, 128), BF16)
    tiles[:, 0] = jnp.zeros((3, WB, 128), BF16)
    tiles[:, ROWS + 1] = jnp.zeros((3, WB, 128), BF16)

    for side, edge in ((0, row == 0), (1, row == ROWS - 1)):
        @pl.when(edge)
        def _():
            feat_in[side] = jnp.zeros((256, WIDTH), BF16)
            raised_in[side] = jnp.zeros((64, WIDTH), BF16)
            feat_rim_in[:, side * (DEP + 1)] = jnp.zeros((2, C1, WIDTH), BF16)
            corner_in[:, side] = jnp.zeros((2, C1, WIDTH), BF16)

    for side, edge in ((0, col == 0), (1, col == COLS - 1)):
        @pl.when(edge)
        def _():
            tiles[2 * side] = jnp.zeros((ROWS + 2, WB, 128), BF16)
            feat_rim_in[side] = jnp.zeros((DEP + 2, C1, WIDTH), BF16)
            rim_in[side] = jnp.zeros((64, WIDTH), BF16)
            corner_in[side] = jnp.zeros((2, C1, WIDTH), BF16)

    def inside(dr, dc):
        yes = None
        for at, step, count in ((row, dr, ROWS), (col, dc, COLS)):
            if step:
                here = at > 0 if step < 0 else at < count - 1
                yes = here if yes is None else jnp.logical_and(yes, here)
        return yes

    def off_seam(dr):
        return row != SEAM - 1 if dr > 0 else row != SEAM

    class Shift:
        def __init__(self, src, dst, send, recv, dr, dc, seam=None):
            self.there, self.back = inside(dr, dc), inside(-dr, -dc)
            if seam is not None:
                self.there = jnp.logical_and(self.there, off_seam(dr))
                self.back = jnp.logical_and(self.back, off_seam(-dr))
            self.copy = pltpu.make_async_remote_copy(
                src_ref=src, dst_ref=dst, send_sem=send, recv_sem=recv,
                device_id=device((row + dr + ROWS) % ROWS, (col + dc + COLS) % COLS), device_id_type=MESH,
            )

        def start(self, also=None):
            @pl.when(self.there if also is None else jnp.logical_and(self.there, also))
            def _():
                self.copy.start()

        def wait(self):
            @pl.when(self.there)
            def _():
                self.copy.wait_send()

            @pl.when(self.back)
            def _():
                self.copy.wait_recv()

    loads[0].wait()
    r_, c_ = iota((128, 256), 0), iota((128, 256), 1)
    pool_h = ones_where(((r_ % C1) == (c_ // HGT)) & ((r_ // C1) == (c_ % HGT) // 2))
    pool_h = jnp.concatenate([pool_h, pool_h], axis=1)
    r_, c_ = iota((64, WIDTH), 0), iota((64, WIDTH), 1)
    pool_w = jnp.where((c_ // 2) == (r_ % WB) * 4 + r_ // WB, 0.125, 0.0).astype(BF16)
    pooled = []
    for a in range(4):
        pair = feat[2 * a : 2 * a + 2].reshape(512, WIDTH)
        pooled.append(dot_nt(pool_w, dot(pool_h, pair).astype(BF16)).astype(BF16))
    pooled = jnp.concatenate(pooled, axis=1)

    loads[1].wait()
    total = jnp.zeros((WB, CB), F32)
    for c in range(4):
        total += dot(pooled[c * WB : (c + 1) * WB], down[:, c].reshape(512, CB))
    low = silu(total).astype(BF16)
    for k in range(4):
        lowered[k] = low[:, k * 128 : (k + 1) * 128]

    r_, c_ = iota((64, 256), 0), iota((64, 256), 1)
    pick = ones_where(((c_ // HGT) == (r_ % C1)) & ((c_ % HGT) == (r_ // C1) * (HGT - 1)))
    for d in range(DEP):
        rim = dot(pick, feat[d]).astype(BF16)
        feat_rim[0, d] = rim[:C1]
        feat_rim[1, d] = rim[C1:]

    pl.semaphore_wait(barrier, ROWS - 1 + 6)

    for offset in PEERS:
        to = peer(offset)
        pltpu.make_async_remote_copy(
            src_ref=lowered.at[to // 8],
            dst_ref=tiles.at[1, 1 + row],
            send_sem=a_send,
            recv_sem=a_recv,
            device_id=device(to, col),
            device_id_type=MESH,
        ).start()

    sides, ends = ((0, -1), (1, 1)), ((0, -1, 0), (1, 1, DEP - 1))
    feat_moves = [(feat.at[d], feat_in.at[1 - e], dr, 0) for e, dr, d in ends]
    feat_moves += [(feat_rim.at[s], feat_rim_in.at[1 - s, pl.ds(1, DEP)], 0, dc) for s, dc in sides]
    feat_moves += [
        (feat_rim.at[s, d], feat_rim_in.at[1 - s, (1 - e) * (DEP + 1)], dr, dc) for s, dc in sides for e, dr, d in ends
    ]
    feat_sends = [
        Shift(src, dst, f_send.at[i], f_recv.at[i], dr, dc) for i, (src, dst, dr, dc) in enumerate(feat_moves)
    ]
    for copy in feat_sends:
        copy.start()

    weight_sends = []
    for j in range(1, GROUP):
        to = (lane + j) % GROUP
        copy = pltpu.make_async_remote_copy(
            src_ref=weight_piece(to),
            dst_ref=weight_slot(lane),
            send_sem=w_send.at[j - 1],
            recv_sem=w_recv.at[j - 1],
            device_id=device(row - lane + to, col),
            device_id_type=MESH,
        )
        copy.start()
        weight_sends.append(copy)

    tiles[1, 1 + row] = lowered[row // 8]

    loads[2].wait()
    r_, c_ = iota((256, C1), 0), iota((256, C1), 1)
    spread_o = ones_where((r_ // HGT) == c_)
    r_, c_ = iota((C1, 256), 0), iota((C1, 256), 1)
    spread_c = ones_where((c_ // HGT) == r_)
    shift = (iota((256, 256), 1) % HGT) - (iota((256, 256), 0) % HGT)
    h_of = iota((256, C1), 0) % HGT
    for kd in range(3):
        for kw in range(3):
            total = jnp.zeros((256, 256), F32)
            tops = []
            for kh in range(3):
                taps = dot_nt(spread_o, dec[(kd * 3 + kh) * 3 + kw]).astype(BF16)
                total = jnp.where(shift == kh - 1, dot(taps, spread_c), total)
                if kh != 1:
                    edge = 0 if kh == 0 else HGT - 1
                    tops.append(jnp.where(h_of == edge, taps.astype(F32), 0.0))
            at = kd * 3 + kw
            band[:, at * 256 : (at + 1) * 256] = total.astype(BF16)
            band_h[:, at * 64 : (at + 1) * 64] = jnp.concatenate(tops, axis=1).astype(BF16)

    def all_tiles(ref, send, recv):
        span = ref.at[pl.ds(1, ROWS - 1)]
        return pltpu.make_async_remote_copy(
            src_ref=span, dst_ref=span, send_sem=send, recv_sem=recv,
            device_id=device(peer(PEERS[0]), col), device_id_type=MESH,
        )

    all_tiles(tiles.at[1], a_send, a_recv).wait_recv()

    halo_sends = []
    for i, (start, size) in enumerate((((1 - row_z) * 15, 17), (row_z * 17, 15))):
        span = pl.ds(1 + start, size)
        halo_sends.append(
            [
                Shift(tiles.at[1, span], tiles.at[1 - dc, span], h_send.at[i, s], h_recv.at[i, s], 0, dc)
                for s, dc in enumerate((-1, 1))
            ]
        )
    for pair in halo_sends:
        for copy in pair:
            copy.start()

    own_weight.wait()
    for copy in weight_sends:
        copy.wait()

    def patches(heights, start):
        return jnp.concatenate(
            [tiles[b, pl.ds(start + a, 16)].reshape(256, 128) for a in range(3) for b in heights], axis=1
        )

    def taps_of(heights):
        return jnp.concatenate(
            [
                jnp.concatenate([wg[a * 9 + b * 3 + c] for a in range(3) for b in heights], axis=0)
                for c in range(3)
            ],
            axis=1,
        )

    def beyond_copy(i, to):
        return pltpu.make_async_remote_copy(
            src_ref=part.at[2 * SEAM - 1 - to], dst_ref=beyond.at[row],
            send_sem=b_send.at[i], recv_sem=b_recv, device_id=device(to, col), device_id_type=MESH,
        )

    starts = ((1 - row_z) * 16, row_z * 16)
    inner_taps = taps_of((1,))
    inner = [dot(patches((1,), start), inner_taps) for start in starts]
    w_of = iota((256, 128), 0) % WB
    for dz, start in ((1, starts[0]), (0, starts[1])):
        for copy in halo_sends[1 - dz]:
            copy.wait()
        partial = inner[1 - dz] + dot(patches((0, 2), start), taps_of((0, 2)))
        before = pltpu.roll(partial[:, :128], 1, 0)
        after = pltpu.roll(partial[:, 256:], 255, 0)
        summed = partial[:, 128:256] + jnp.where(w_of == 0, 0.0, before) + jnp.where(w_of == WB - 1, 0.0, after)
        part[pl.ds(start, 16)] = summed.astype(BF16).reshape(16, WB, 128)
        if dz == 0:
            for i, to in enumerate((SEAM, SEAM - 1)):
                @pl.when(row != to)
                def _():
                    beyond_copy(i, to).start()

                @pl.when(row == to)
                def _():
                    beyond[row] = part[2 * SEAM - 1 - to]

        for offset in PEERS:
            if offset[0] == dz:
                to = peer(offset)
                pltpu.make_async_remote_copy(
                    src_ref=part.at[to],
                    dst_ref=arrived.at[row],
                    send_sem=p_send,
                    recv_sem=p_recv,
                    device_id=device(to, col),
                    device_id_type=MESH,
                ).start()

    arrived[row] = part[row]
    r_, c_ = iota((WB, 512), 1), iota((WB, 512), 0)
    spread_w = ones_where((((r_ % WIDTH) // 8) == c_) & ((((r_ % WIDTH) // 2) % 4) == (r_ // WIDTH)))
    r_, c_ = iota((256, 128), 0), iota((256, 128), 1)
    raise_h = ones_where(((c_ % C1) == (r_ // HGT)) & ((c_ // C1) == (r_ % HGT) // 2))
    loads[3].wait()
    all_tiles(arrived, p_send, p_recv).wait_recv()

    def spread_of(shares):
        groups = shares.reshape(ROWS // GROUP, GROUP, WB, 128).astype(F32).sum(axis=0)
        middle = silu(jnp.concatenate([groups[k] for k in range(GROUP)], axis=1)).astype(BF16)
        across = lax.dot_general(middle, spread_w, (((0,), (0,)), ((), ())), preferred_element_type=F32)
        across = across.astype(BF16)
        return jnp.concatenate([across[:, c * WIDTH : (c + 1) * WIDTH] for c in range(4)], axis=0)

    def raised_layers(layers, spread):
        rows = [
            jnp.concatenate([up[a * 4 : a * 4 + 4, c].reshape(128, CB) for a in layers], axis=0) for c in range(4)
        ]
        return dot(jnp.concatenate(rows, axis=1), spread)

    odd = (iota((64, WIDTH), 1) % 2) == 1

    def packed(value):
        return jnp.where(odd, value[64:], value[:64]).astype(BF16)

    def unpacked(value):
        both = value.astype(F32)
        even_rows = jnp.where(odd, pltpu.roll(both, 1, 1), both)
        odd_rows = jnp.where(odd, both, pltpu.roll(both, WIDTH - 1, 1))
        return jnp.concatenate([even_rows, odd_rows], axis=0)

    spread = spread_of(arrived[...])
    raised = [None] * 4
    joined_sends = []

    def send(src, dst, dr, dc, seam=None):
        i = len(joined_sends)
        joined_sends.append(Shift(src, dst, j_send.at[i], j_recv.at[i], dr, dc, seam))
        joined_sends[-1].start()

    outer = raised_layers((0, 3), spread)
    raised[0], raised[3] = outer[:128], outer[128:]
    for e, dr, a in ((0, -1, 0), (1, 1, 3)):
        raised_out[e] = packed(raised[a])
        send(raised_out.at[e], raised_in.at[1 - e], dr, 0, False)
        for s, dc in sides:
            corner_out[s, e] = raised[a][96 * s : 96 * s + C1].astype(BF16)
            send(corner_out.at[s, e], corner_in.at[1 - s, 1 - e], dr, dc, False)
    inner = raised_layers((1, 2), spread)
    raised[1], raised[2] = inner[:128], inner[128:]
    for s, dc in sides:
        rim_out[s] = packed(jnp.concatenate([raised[a][96 * s : 96 * s + C1] for a in range(4)], axis=0))
        send(rim_out.at[s], rim_in.at[1 - s], 0, dc)

    for copy in feat_sends:
        copy.wait()

    for e, here, dr in ((0, SEAM, -1), (1, SEAM - 1, 1)):
        @pl.when(row == here)
        def _():
            all_tiles(beyond, b_send.at[0], b_recv).wait_recv()
            layer = raised_layers((3 * (1 - e),), spread_of(beyond[...]))
            raised_in[e] = packed(layer)
            for s in range(2):
                corner_out[s, 2 + e] = layer[96 * s : 96 * s + C1].astype(BF16)

    for e, here in ((0, SEAM), (1, SEAM - 1)):
        for s, dc in sides:
            copy = Shift(
                corner_out.at[s, 2 + e], corner_in.at[1 - s, e], s_send.at[s, e], s_recv.at[s, e], 0, dc
            )
            copy.there = jnp.logical_and(copy.there, row == here)
            copy.back = jnp.logical_and(copy.back, row == here)
            copy.start()
            joined_sends.append(copy)

    v_of = iota((256, WIDTH), 1)

    def shifted(value):
        v_ = v_of[: value.shape[0]]
        value = value.astype(F32)
        return (
            jnp.where(v_ == 0, 0.0, pltpu.roll(value, 1, 1)).astype(BF16),
            jnp.where(v_ == WIDTH - 1, 0.0, pltpu.roll(value, WIDTH - 1, 1)).astype(BF16),
        )

    def store_slab(i, layer, lift):
        joined = (layer.astype(F32) + lift).astype(BF16)
        slabs[i, 1] = joined
        slabs[i, 0], slabs[i, 2] = shifted(joined)

    for d in range(DEP):
        if d % 2 == 0:
            lift = dot(raise_h, raised[d // 2].astype(BF16))
        store_slab(1 + d, feat[d], lift)

    def windows(ref, d, first, last, size):
        return jnp.concatenate(
            [ref[d + i + first : d + i + last].reshape((last - first) * 3 * size, WIDTH) for i in range(2)], axis=1
        )

    spans = ((1, 3), (0, 3), (0, 3), (0, 2))
    for p, (first, last) in enumerate(spans):
        accs[p] = dot(band[:, first * 768 : last * 768], windows(slabs, 2 * p, first, last, 256))

    def store_rim(d, lifts):
        rim = [(feat_rim_in[s, d].astype(F32) + lifts[s]).astype(BF16) for s in range(2)]
        rim = jnp.concatenate(rim, axis=0)
        edges[d, 1] = rim
        edges[d, 0], edges[d, 2] = shifted(rim)

    def finish(p):
        total = accs[p] + dot(band_h[...], windows(edges, 2 * p, 0, 3, 64))
        if p == 0:
            total += dot(band[:, :768], windows(slabs, 0, 0, 1, 256))
        if p == 3:
            total += dot(band[:, 1536:], windows(slabs, 6, 2, 3, 256))
        total = silu(total).astype(BF16)
        out_ref[2 * p] = total[:, :WIDTH]
        out_ref[2 * p + 1] = total[:, WIDTH:]

    for copy in joined_sends[6:8]:
        copy.wait()
    rims = [unpacked(rim_in[s]) for s in range(2)]
    for d in range(DEP):
        a = d // 2
        store_rim(1 + d, [rims[s][a * C1 : (a + 1) * C1] for s in range(2)])
    for p in (1, 2):
        finish(p)

    for copy in joined_sends[:6] + joined_sends[8:]:
        copy.wait()
    for e in range(2):
        store_slab(e * (DEP + 1), feat_in[e], dot(raise_h, unpacked(raised_in[e]).astype(BF16)))
        store_rim(e * (DEP + 1), [corner_in[s, e].astype(F32) for s in range(2)])
    for p in (0, 3):
        finish(p)

    all_tiles(tiles.at[1], a_send, a_recv).wait_send()
    all_tiles(arrived, p_send, p_recv).wait_send()
    for i, to in enumerate((SEAM, SEAM - 1)):
        @pl.when(row != to)
        def _():
            beyond_copy(i, to).wait_send()


def body(features, down_weight, bott_weight, up_weight, dec_weight):
    dma = pltpu.SemaphoreType.DMA
    out = pl.pallas_call(
        kernel,
        out_shape=jax.ShapeDtypeStruct((DEP, 256, WIDTH), BF16),
        in_specs=[pl.BlockSpec(memory_space=pltpu.HBM)] * 5,
        out_specs=pl.BlockSpec(memory_space=pltpu.VMEM),
        scratch_shapes=[
            pltpu.VMEM((DEP, 256, WIDTH), BF16),
            pltpu.VMEM((16, 4, C1, CB), BF16),
            pltpu.VMEM((16, 4, C1, CB), BF16),
            pltpu.VMEM((27, C1, C1), BF16),
            pltpu.VMEM((27, 128, 128), BF16),
            pltpu.VMEM((4, WB, 128), BF16),
            pltpu.VMEM((3, ROWS + 2, WB, 128), BF16),
            pltpu.VMEM((ROWS, WB, 128), BF16),
            pltpu.VMEM((ROWS, WB, 128), BF16),
            pltpu.VMEM((256, 9 * 256), BF16),
            pltpu.VMEM((256, 9 * 64), BF16),
            pltpu.VMEM((DEP + 2, 3, 256, WIDTH), BF16),
            pltpu.VMEM((DEP + 2, 3, 64, WIDTH), BF16),
            pltpu.VMEM((DEP // 2, 256, 2 * WIDTH), F32),
            pltpu.VMEM((2, 256, WIDTH), BF16),
            pltpu.VMEM((2, DEP, C1, WIDTH), BF16),
            pltpu.VMEM((2, DEP + 2, C1, WIDTH), BF16),
            pltpu.VMEM((ROWS, WB, 128), BF16),
            pltpu.VMEM((2, 64, WIDTH), BF16),
            pltpu.VMEM((2, 64, WIDTH), BF16),
            pltpu.VMEM((2, 64, WIDTH), BF16),
            pltpu.VMEM((2, 64, WIDTH), BF16),
            pltpu.VMEM((2, 4, C1, WIDTH), BF16),
            pltpu.VMEM((2, 2, C1, WIDTH), BF16),
            dma((5,)), dma((6,)), dma((6,)), dma, dma, dma((2, 2)), dma((2, 2)), dma, dma, dma((2,)), dma,
            dma((8,)), dma((8,)), dma((8,)), dma((8,)), dma((2, 2)), dma((2, 2)),
        ],
        compiler_params=pltpu.CompilerParams(
            collective_id=0, has_side_effects=True, vmem_limit_bytes=60 * 1024 * 1024
        ),
        name="encode_decode",
    )(
        features.reshape(DEP, 256, WIDTH),
        down_weight.reshape(16, 4, C1, CB),
        bott_weight.reshape(27, CIN, CB),
        up_weight.reshape(16, 4, C1, CB),
        dec_weight.reshape(27, C1, C1),
    )
    return out.reshape(features.shape)


def solution(mesh):
    placed = (P("row", None, "col", None), P(), P(None, None, None, "row", None), P(), P())
    return jax.shard_map(
        body, mesh=mesh, in_specs=placed, out_specs=P("row", None, "col", None), check_vma=False
    )
```
